512 devices in a mesh: grp: 16 (over z, core), ex: 32 (over y, x).
Axes of the slice: x: 4, y: 8, z: 8, core: 2. Of those that a mesh axis runs over, the one named last changes fastest.
Arguments:
- tokens: bfloat16 [8192, 2880], P('ex', 'grp'), may hold values from -6 to 6
- out_grad: bfloat16 [8192, 2880], P('ex', 'grp'), may hold values from -6 to 6
- expert_ids: int32 [8192, 4], P('ex'), may hold values from 0 to 127, all different within a row; in each aligned block of 256 rows (0 to 255, 256 to 511, ...) at most 16 rows name the same one
- gate_values: bfloat16 [8192, 4], P('ex'), may hold values from 0.049804688 to 0.59765625
- w_gate: bfloat16 [32, 2880, 2880], P('ex', 'grp'), may hold values from -0.109375 to 0.109375
- w_up: bfloat16 [32, 2880, 2880], P('ex', 'grp'), may hold values from -0.109375 to 0.109375
- w_down: bfloat16 [32, 2880, 2880], P('ex', 'grp'), may hold values from -0.109375 to 0.109375
Outputs:
- token_grad: bfloat16 [8192, 2880], P('ex', 'grp')
- gate_grad: float32 [8192, 4], P('ex')
The draws below stay inside these ranges and needn't reach their ends.
Inputs may be any that keep to these rules, and one draw needn't show every extreme that they name: `expert_ids`: each row names 4 different experts. Among the rows of one index of ex no expert is named more than 16 times, a bound that some block reaches there.
All inputs are finite; a program needn't handle non-finite values.
Results may differ from the reference program's by a relative error of at most 0.019.
Values may be sent and summed in bfloat16 or wider, within the bound.
No kernel may reach another device: no remote copies, remote signals or barrier semaphores. Data moves between devices by JAX's collectives and lax.ppermute only.
A program may use at most 64 MiB of HBM per device.

```python
import math
import jax
import jax.numpy as jnp
import numpy as np
from jax import lax

D = 2880
FF = 2880
EXPERTS = 128
TOP = 4
TOK_DEV = 256
CAP = 16
WIN = 32
TOKENS = 8192
N_GRP = 16
N_EX = 32


def block_levels(key, shape, pieces, smallest, top_value):
    loudness = 1.0
    for dim, parts in pieces:
        steps = jax.random.uniform(jax.random.fold_in(jax.random.fold_in(key, 6), dim), (parts,), jnp.float32, smallest / len(pieces), top_value / len(pieces))
        loudness = loudness * jnp.repeat(jnp.exp(steps), shape[dim] // parts).reshape((-1,) + (1,) * (len(shape) - 1 - dim))
    return loudness


def deal_out(rng, own, number, rows, count, top, bound, lean):
    ranking = jax.random.permutation(rng, count)
    heavy_load, usual = portions_of(count, rows * top, bound, lean, True), portions_of(count, rows * top, bound, lean, False)
    places = jnp.arange(count)

    def named(tallies, rotation):
        used = int((tallies > 0).sum())
        fixed = max(1, used // 4)
        passed = fixed + (places - fixed + rotation * (used - fixed)) % max(1, count - fixed)
        return jnp.zeros((count,), jnp.int32).at[ranking[jnp.where(places < fixed, places, passed)]].set(jnp.asarray(tallies, jnp.int32))

    tallies = jnp.where(number % 4 == 0, named(heavy_load, number // 4), named(usual, number - number // 4 - 1))
    mixed = jax.random.permutation(jax.random.fold_in(own, 3), count)
    source_of, receiver = mixed[0:count // 2 * 2:2], mixed[1:count // 2 * 2:2]
    margin = jnp.minimum(tallies[source_of] - 1, bound - tallies[receiver]) // 2
    margin = jnp.where((source_of == ranking[0]) | (receiver == ranking[0]) | (tallies[receiver] == 0), 0, jnp.maximum(margin, 0))
    passed = jax.random.randint(jax.random.fold_in(own, 4), (count // 2,), 0, 1 << 20) % (margin + 1)
    tallies = tallies.at[source_of].add(-passed).at[receiver].add(passed)
    labels = jnp.searchsorted(jnp.cumsum(tallies), jnp.arange(rows * top), side="right").astype(jnp.int32)
    listing = labels.reshape(top, rows).T
    listing = listing[jax.random.permutation(jax.random.fold_in(own, 1), rows)]
    rotation = jax.random.randint(jax.random.fold_in(own, 2), (rows, 1), 0, top)
    return jnp.take_along_axis(listing, (jnp.arange(top)[None, :] + rotation) % top, axis=1)


def portions_of(amount, total, most, skew, full):
    portions = [(1 << 20) // math.isqrt(standing ** skew) + 1 for standing in range(1, amount + 1)]
    largest = most if full else min(most, max(-(-total // amount), total * portions[0] // sum(portions)))
    least = 1 if total - largest >= amount - 1 else 0
    given, rest = [largest] + [least] * (amount - 1), total - largest - least * (amount - 1)
    while rest > 0:
        free = [i for i in range(1, amount) if given[i] < largest] or [i for i in range(1, amount) if given[i] < most]
        whole, remaining = sum([portions[i] for i in free]), rest
        for i in free:
            more = min(most - given[i], max(1, remaining * portions[i] // whole), rest)
            given[i] = given[i] + more
            rest = rest - more
    return np.array(given)


def normal_values(key, extent, scale, bound, shards=(), held_as=jnp.bfloat16):
    loudness = block_levels(key, extent, shards, -0.22, 0.18) if shards else 1.0
    entries = jax.random.normal(key, extent, jnp.float32) * scale * loudness
    return jnp.minimum(jnp.maximum(entries, -bound), bound).astype(held_as)


def setup_inputs(seed: int = 0) -> dict:
    key_list = jax.random.split(jax.random.key(seed), 8)
    tokens = normal_values(key_list[0], (TOKENS, D), 1.0, 6.0, ((0, 32), (1, 16)))
    out_grad = normal_values(key_list[1], (TOKENS, D), 1.0, 6.0, ((0, 32), (1, 16)))
    expert_ids_keys = jax.random.split(jax.random.fold_in(key_list[2], 1), TOKENS // TOK_DEV)
    expert_ids_turns = jax.random.permutation(jax.random.fold_in(key_list[2], 3), TOKENS // TOK_DEV)
    expert_ids = jax.vmap(lambda own, number: deal_out(jax.random.fold_in(key_list[2], 2), own, number, TOK_DEV, EXPERTS, TOP, CAP, 2))(expert_ids_keys, expert_ids_turns).reshape((TOKENS, TOP))
    gate_values = jnp.clip(jnp.exp(math.log(0.59765625) - 2.4849066 * jax.random.uniform(key_list[3], (TOKENS, TOP), jnp.float32) ** block_levels(key_list[3], (TOKENS, TOP), ((0, 32),), -0.2, 0.2)), 0.049804688, 0.59765625).astype(jnp.bfloat16)
    w_gate = normal_values(key_list[4], (WIN, FF, D), D ** -0.5, 0.109375, ((0, 32), (1, 16)))
    w_up = normal_values(key_list[5], (WIN, FF, D), D ** -0.5, 0.109375, ((0, 32), (1, 16)))
    w_down = normal_values(key_list[6], (WIN, FF, D), FF ** -0.5, 0.109375, ((0, 32), (1, 16)))
    return {"tokens": tokens, "out_grad": out_grad, "expert_ids": expert_ids, "gate_values": gate_values, "w_gate": w_gate, "w_up": w_up, "w_down": w_down}


def reference(tokens, out_grad, expert_ids, gate_values, w_gate, w_up, w_down):
    slots = N_EX * CAP
    group = FF // N_GRP
    highest = lax.Precision.HIGHEST

    def one_expert(carry, expert):
        token_acc, gate_acc = carry
        member = expert_ids == expert
        hit = jnp.any(member, axis=1)
        rows = jnp.nonzero(hit, size=slots, fill_value=0)[0].astype(jnp.int32)
        live = jnp.arange(slots) < jnp.sum(hit.astype(jnp.int32))
        picked = jnp.where(live[:, None], tokens[rows], jnp.zeros((), jnp.bfloat16))
        grads = jnp.where(live[:, None], out_grad[rows], jnp.zeros((), jnp.bfloat16))
        weight = jnp.sum(jnp.where(member, gate_values.astype(jnp.float32), 0.0), axis=1)[rows]
        weight = jnp.where(live, weight, 0.0)
        wgate = w_gate[expert]
        wup = w_up[expert]
        wdown = w_down[expert]
        dims = (((1,), (1,)), ((), ()))
        pre_gate = lax.dot_general(picked, wgate, dims, preferred_element_type=jnp.float32)
        pre_up = lax.dot_general(picked, wup, dims, preferred_element_type=jnp.float32)
        back = lax.dot_general(grads, wdown, dims, preferred_element_type=jnp.float32)
        sig = jax.nn.sigmoid(pre_gate)
        act = pre_gate * sig
        hidden = act * pre_up
        prob_grad = jnp.sum(back * hidden, axis=1)
        hid_grad = weight[:, None] * back
        d_gate = (hid_grad * pre_up * sig * (1.0 + pre_gate * (1.0 - sig))).astype(jnp.bfloat16)
        d_up = (hid_grad * act).astype(jnp.bfloat16)
        dg3 = d_gate.astype(jnp.float32).reshape(slots, N_GRP, group)
        du3 = d_up.astype(jnp.float32).reshape(slots, N_GRP, group)
        wg3 = wgate.astype(jnp.float32).reshape(N_GRP, group, D)
        wu3 = wup.astype(jnp.float32).reshape(N_GRP, group, D)
        terms = jnp.einsum("rgf,gfd->rgd", dg3, wg3, precision=highest)
        terms = terms + jnp.einsum("rgf,gfd->rgd", du3, wu3, precision=highest)
        terms = lax.optimization_barrier(terms.astype(jnp.bfloat16)).astype(jnp.float32)
        partial_sum = jnp.sum(terms, axis=1)
        partial_sum = jnp.where(live[:, None], partial_sum, 0.0)
        token_acc = token_acc.at[rows].add(partial_sum)
        prob_token = jnp.zeros((TOKENS,), jnp.float32).at[rows].add(jnp.where(live, prob_grad, 0.0))
        gate_acc = gate_acc + jnp.where(member, prob_token[:, None], 0.0)
        return (token_acc, gate_acc), None

    start = (jnp.zeros((TOKENS, D), jnp.float32), jnp.zeros((TOKENS, TOP), jnp.float32))
    (token_acc, gate_acc), _ = lax.scan(one_expert, start, jnp.arange(N_EX, dtype=jnp.int32))
    return token_acc.astype(jnp.bfloat16), gate_acc
```

```python
import jax
import jax.numpy as jnp
from jax import lax
from jax.experimental import pallas as pl
from jax.experimental.pallas import tpu as pltpu
from jax.sharding import PartitionSpec as P

TOP = 4
CAP = 16
FEATS = 180
HIDDEN = 180
BLOCKS = 7
SEND = 384
HID = 192
NT = (((1,), (1,)), ((), ()))
TN = (((0,), (0,)), ((), ()))
F32 = jnp.float32
BF16 = jnp.bfloat16


def dispatch_kernel(ids_ref, gate_ref, feat_ref, rows_ref, sel_ref):
    experts = rows_ref.shape[0] // CAP
    count = ids_ref.shape[1]
    gates = gate_ref[...].astype(F32)
    expert = lax.broadcasted_iota(jnp.int32, (experts, count), 0)
    member = jnp.zeros((experts, count), F32)
    weight = jnp.zeros((experts, count), F32)
    for k in range(TOP):
        named = ids_ref[k : k + 1, :] == expert
        member = jnp.where(named, 1.0, member)
        weight = jnp.where(named, gates[k : k + 1, :], weight)
    earlier = lax.broadcasted_iota(jnp.int32, (count, count), 0) < lax.broadcasted_iota(
        jnp.int32, (count, count), 1
    )
    place = jnp.dot(
        member.astype(BF16), earlier.astype(F32).astype(BF16), preferred_element_type=F32
    )
    code = jnp.where(member > 0.0, place, -1.0)
    slot = lax.broadcasted_iota(jnp.int32, (experts, CAP, count), 1).astype(F32)
    picked = code[:, None, :] == slot
    select = jnp.where(picked, 1.0, 0.0).reshape(experts * CAP, count).astype(BF16)
    slot_weight = jnp.sum(
        jnp.where(picked, weight[:, None, :], 0.0).reshape(experts * CAP, count),
        axis=1,
        keepdims=True,
    )
    sel_ref[...] = select
    rows = lax.dot_general(select, feat_ref[...], NT, preferred_element_type=F32)
    lane = lax.broadcasted_iota(jnp.int32, rows.shape, 1)
    rows_ref[...] = jnp.where(lane == 2 * FEATS, slot_weight, rows).astype(BF16)


def expert_kernel(rows_ref, w1_ref, w3_ref, w2_ref, out_ref, acc_ref, grad_ref):
    step = pl.program_id(0)
    groups = pl.num_programs(0) - BLOCKS

    @pl.when(step == 0)
    def _():
        acc_ref[...] = jnp.zeros_like(acc_ref)

    @pl.when(step < groups)
    def _():
        rows = rows_ref[0]
        acc_ref[: 2 * HID, :] += lax.dot_general(
            w1_ref[0], rows[:, :256], NT, preferred_element_type=F32
        )
        acc_ref[2 * HID :, :] += lax.dot_general(
            w3_ref[0], rows[:, 128:], NT, preferred_element_type=F32
        )

    @pl.when(step == groups - 1)
    def _():
        hid = HIDDEN
        pre_gate = acc_ref[:HID, :]
        pre_up = acc_ref[HID : 2 * HID, :]
        back = acc_ref[2 * HID :, :]
        weight = acc_ref[2 * HID + hid : 2 * HID + hid + 1, :]
        sig = jax.nn.sigmoid(pre_gate)
        act = pre_gate * sig
        prob = jnp.sum(back * (act * pre_up), axis=0, keepdims=True)
        hid_grad = weight * back
        d_gate = hid_grad * pre_up * sig * (1.0 + pre_gate * (1.0 - sig))
        d_up = hid_grad * act
        high = prob.astype(BF16).astype(F32)
        row = lax.broadcasted_iota(jnp.int32, d_gate.shape, 0)
        d_gate = jnp.where(row < hid, d_gate, 0.0)
        d_gate = jnp.where(row == hid, high, d_gate)
        d_gate = jnp.where(row == hid + 1, prob - high, d_gate)
        grad_ref[:HID, :] = d_gate.astype(BF16)
        grad_ref[HID:, :] = jnp.where(row < hid, d_up, 0.0).astype(BF16)

    @pl.when(step >= groups)
    def _():
        out_ref[...] = jnp.dot(
            w2_ref[...], grad_ref[...], preferred_element_type=F32
        ).astype(BF16)


def combine_kernel(ret_ref, sel_ref, ids_ref, tok_ref, gate_ref):
    feats, count = tok_ref.shape
    slots = sel_ref.shape[0]
    experts = slots // CAP
    ret = ret_ref[...]
    total = lax.dot_general(ret, sel_ref[...], TN, preferred_element_type=F32)
    tok_ref[...] = total[:feats, :].astype(BF16)
    prob = ret[:, feats : feats + 1].astype(F32) + ret[:, feats + 1 : feats + 2].astype(F32)
    spread = (sel_ref[...].astype(F32) * prob).reshape(experts, CAP, count)
    per_expert = jnp.sum(spread, axis=1)
    expert = lax.broadcasted_iota(jnp.int32, (experts, count), 0)
    for k in range(TOP):
        named = ids_ref[k : k + 1, :] == expert
        gate_ref[k : k + 1, :] = jnp.sum(
            jnp.where(named, per_expert, 0.0), axis=0, keepdims=True
        )


def pack_first(w, groups, lead, rows):
    hid, width = w.shape
    feats = width // groups
    w = w.reshape(hid, groups, feats).transpose(1, 0, 2)
    return jnp.pad(w, ((0, 0), (0, rows - hid), (lead, 256 - feats - lead)))


def pack_second(w, groups):
    hid, width = w.shape
    feats = width // groups
    w = w.T.reshape(groups, feats, hid)
    return jnp.pad(w, ((0, 0), (0, 2), (0, HID - hid)))


def per_device(tokens, out_grad, expert_ids, gate_values, w_gate, w_up, w_down):
    experts = lax.axis_size("ex")
    groups = lax.axis_size("grp")
    slots = experts * CAP
    count, feats = tokens.shape
    hid = w_gate.shape[1]
    ids = expert_ids.T
    gates = gate_values.T
    feat = jnp.concatenate(
        [tokens.T, out_grad.T, jnp.zeros((SEND - 2 * feats, count), BF16)], axis=0
    )
    rows, select = pl.pallas_call(
        dispatch_kernel,
        out_shape=(
            jax.ShapeDtypeStruct((slots, SEND), BF16),
            jax.ShapeDtypeStruct((slots, count), BF16),
        ),
        name="dispatch",
    )(ids, gates, feat)
    rows = lax.all_to_all(
        rows.reshape(experts, CAP, SEND), "ex", split_axis=0, concat_axis=0, tiled=True
    ).reshape(slots, SEND)
    all_rows = lax.all_gather(rows, "grp")

    w1 = jnp.concatenate(
        [pack_first(w_gate[0], groups, 0, HID), pack_first(w_up[0], groups, 0, HID)], axis=1
    )
    w3 = pack_first(w_down[0], groups, 2 * feats - 128 - feats, HID)
    w3 = w3.at[0, hid, 2 * feats - 128].set(1.0)
    w2 = jnp.concatenate([pack_second(w_gate[0], groups), pack_second(w_up[0], groups)], axis=2)
    w2 = w2.at[:, feats, hid].set(1.0).at[:, feats + 1, hid + 1].set(1.0)
    chunk = feats + 2
    w2 = w2.reshape(groups * chunk, 2 * HID)
    block = groups * chunk // BLOCKS
    terms = pl.pallas_call(
        expert_kernel,
        grid=(groups + BLOCKS,),
        in_specs=[
            pl.BlockSpec((1, slots, SEND), lambda i: (jnp.minimum(i, groups - 1), 0, 0)),
            pl.BlockSpec((1, 2 * HID, 256), lambda i: (jnp.minimum(i, groups - 1), 0, 0)),
            pl.BlockSpec((1, HID, 256), lambda i: (jnp.minimum(i, groups - 1), 0, 0)),
            pl.BlockSpec((block, 2 * HID), lambda i: (jnp.maximum(i - groups, 0), 0)),
        ],
        out_specs=pl.BlockSpec((block, slots), lambda i: (jnp.maximum(i - groups, 0), 0)),
        out_shape=jax.ShapeDtypeStruct((groups * chunk, slots), BF16),
        scratch_shapes=[
            pltpu.VMEM((3 * HID, slots), F32),
            pltpu.VMEM((2 * HID, slots), BF16),
        ],
        compiler_params=pltpu.CompilerParams(vmem_limit_bytes=24 * 1024 * 1024),
        name="expert",
    )(all_rows, w1, w3, w2)

    part = lax.psum_scatter(terms, "grp", scatter_dimension=0, tiled=True)
    ret = lax.all_to_all(
        part.T.reshape(experts, CAP, chunk), "ex", split_axis=0, concat_axis=0, tiled=True
    ).reshape(slots, chunk)
    tok, gate = pl.pallas_call(
        combine_kernel,
        out_shape=(
            jax.ShapeDtypeStruct((feats, count), BF16),
            jax.ShapeDtypeStruct((TOP, count), F32),
        ),
        name="combine",
    )(ret, select, ids)
    return tok.T, gate.T


def solution(mesh):
    return jax.shard_map(
        per_device,
        mesh=mesh,
        in_specs=(
            P("ex", "grp"),
            P("ex", "grp"),
            P("ex", None),
            P("ex", None),
            P("ex", "grp", None),
            P("ex", "grp", None),
            P("ex", "grp", None),
        ),
        out_specs=(P("ex", "grp"), P("ex", None)),
        check_vma=False,
    )
```

```python
import jax
import jax.numpy as jnp
from jax import lax
from jax.experimental import pallas as pl
from jax.experimental.pallas import tpu as pltpu
from jax.sharding import PartitionSpec as P

TOP = 4
CAP = 16
HALF = CAP // 2
FEATS = 180
HIDDEN = 180
HID = 192
WIDE = 384
CHIP = 2 * FEATS
NT = (((1,), (1,)), ((), ()))
TN = (((0,), (0,)), ((), ()))
F32 = jnp.float32
BF16 = jnp.bfloat16


def iota(shape, dim):
    return lax.broadcasted_iota(jnp.int32, shape, dim)


def dispatch_kernel(core_ref, ids_ref, gate_ref, own_ref, peer_ref, rows_ref, sel_ref, feat_ref):
    slots, count = sel_ref.shape
    experts = slots // HALF
    core = core_ref[0]
    gates = gate_ref[...].astype(F32)
    expert = iota((experts, count), 0)
    member = jnp.zeros((experts, count), F32)
    weight = jnp.zeros((experts, count), F32)
    for k in range(TOP):
        named = ids_ref[k : k + 1, :] == expert
        member = jnp.where(named, 1.0, member)
        weight = jnp.where(named, gates[k : k + 1, :], weight)
    earlier = jnp.where(iota((count, count), 0) < iota((count, count), 1), 1.0, 0.0)
    place = jnp.dot(member.astype(BF16), earlier.astype(BF16), preferred_element_type=F32)
    code = jnp.where(member > 0.0, place - (HALF * core).astype(F32), -1.0)
    picked = code[:, None, :] == iota((experts, HALF, count), 1).astype(F32)
    select = jnp.where(picked, 1.0, 0.0).reshape(slots, count).astype(BF16)
    slot_weight = jnp.sum(
        jnp.where(picked, weight[:, None, :], 0.0).reshape(slots, count), axis=1, keepdims=True
    )
    sel_ref[...] = select
    feat_ref[...] = jnp.zeros_like(feat_ref)
    for part in range(2):
        own = own_ref[part].astype(F32)
        peer = peer_ref[part].astype(F32)
        base = part * WIDE
        feat_ref[base : base + FEATS, :] = jnp.where(core == 0, own, peer)
        feat_ref[base + FEATS : base + CHIP, :] = jnp.where(core == 0, peer, own)
    rows = lax.dot_general(
        select, feat_ref[...].astype(BF16), NT, preferred_element_type=F32
    )
    rows_ref[...] = jnp.where(iota(rows.shape, 1) == CHIP, slot_weight, rows).astype(BF16)


def pack_kernel(gate_ref, up_ref, down_ref, out_ref):
    chips = out_ref.shape[0]
    spare = HID - HIDDEN
    spot = iota((spare, WIDE), 1) == iota((spare, WIDE), 0) + CHIP
    mark = jnp.where(jnp.logical_and(spot, iota((spare, WIDE), 0) < 2), 1.0, 0.0)
    lane = iota((HID, WIDE), 1)
    for chip in range(chips):
        start = chip * CHIP
        low = start // 128 * 128
        high = min(low + 512, gate_ref.shape[1])
        for part, ref in enumerate((gate_ref, up_ref, down_ref)):
            w = ref[:, low:high].astype(F32)
            w = w[:, start - low : start - low + CHIP]
            w = jnp.concatenate([w, jnp.zeros((HIDDEN, WIDE - CHIP), F32)], axis=1)
            tail = mark if part == 0 else jnp.zeros_like(mark)
            w = jnp.concatenate([w, tail], axis=0)
            out_ref[chip, part * HID : (part + 1) * HID, :] = w.astype(BF16)


def expert_kernel(order_ref, *refs):
    blocks, last = refs[:7], refs[7:9]
    own_w, peer_w, out_ref, own_acc, peer_acc, own_d, peer_d, terms = refs[9:]
    step = pl.program_id(0)
    chips = pl.num_programs(0) // 2

    def add(rows):
        for w_ref, acc in ((own_w, own_acc), (peer_w, peer_acc)):
            acc[: 2 * HID, :] += lax.dot_general(
                w_ref[0, : 2 * HID, :], rows[:, :WIDE], NT, preferred_element_type=F32
            )
            acc[2 * HID :, :] += lax.dot_general(
                w_ref[0, 2 * HID :, :], rows[:, WIDE:], NT, preferred_element_type=F32
            )

    @pl.when(step == 0)
    def _():
        own_acc[...] = jnp.zeros_like(own_acc)
        peer_acc[...] = jnp.zeros_like(peer_acc)

    for k in range(7):

        @pl.when(step == k)
        def _(k=k):
            add(blocks[k][...])

    @pl.when(step == 7)
    def _():
        add(jnp.concatenate([last[0][...], last[1][...]], axis=0))
        probs = []
        for acc, grad in ((own_acc, own_d), (peer_acc, peer_d)):
            pre_gate = acc[:HID, :]
            pre_up = acc[HID : 2 * HID, :]
            back = acc[2 * HID :, :]
            weight = acc[HIDDEN : HIDDEN + 1, :] * (1.0 / chips)
            sig = jax.nn.sigmoid(pre_gate)
            act = pre_gate * sig
            live = iota(act.shape, 0) < HIDDEN
            probs.append(
                jnp.sum(jnp.where(live, back * (act * pre_up), 0.0), axis=0, keepdims=True)
            )
            hid_grad = weight * back
            d_gate = hid_grad * pre_up * sig * (1.0 + pre_gate * (1.0 - sig))
            d_up = hid_grad * act
            grad[:HID, :] = jnp.where(live, d_gate, 0.0).astype(BF16)
            grad[HID:, :] = jnp.where(live, d_up, 0.0).astype(BF16)
        prob = probs[0] + probs[1]
        high = prob.astype(BF16).astype(F32)
        spare = iota((16, prob.shape[1]), 0)
        tail = own_d[HID - 16 : HID, :].astype(F32)
        tail = jnp.where(spare == HIDDEN - HID + 16, high, tail)
        tail = jnp.where(spare == HIDDEN - HID + 17, prob - high, tail)
        own_d[HID - 16 : HID, :] = tail.astype(BF16)

    chunk = CHIP + 2
    for k in range(8):

        @pl.when(step == 8 + k)
        def _(k=k):
            value = lax.dot_general(
                own_w[0, : 2 * HID, :], own_d[...], TN, preferred_element_type=F32
            ) + lax.dot_general(
                peer_w[0, : 2 * HID, :], peer_d[...], TN, preferred_element_type=F32
            )
            terms[k * chunk : (k + 1) * chunk, :] = value[:chunk, :]

    @pl.when(step == 15)
    def _():
        out_ref[...] = terms[...].astype(BF16)


def combine_kernel(core_ref, ret_ref, sel_ref, ids_ref, keep_ref, send_ref):
    slots, count = sel_ref.shape
    experts = slots // HALF
    core = core_ref[0]
    ret = ret_ref[...]
    select = sel_ref[...]
    total = lax.dot_general(ret, select, TN, preferred_element_type=F32)
    first, second = total[:FEATS, :], total[FEATS:CHIP, :]
    keep_ref[:FEATS, :] = jnp.where(core == 0, first, second)
    send_ref[:FEATS, :] = jnp.where(core == 0, second, first)
    prob = ret[:, CHIP : CHIP + 1].astype(F32) + ret[:, CHIP + 1 : CHIP + 2].astype(F32)
    per_expert = jnp.sum((select.astype(F32) * prob).reshape(experts, HALF, count), axis=1)
    expert = iota((experts, count), 0)
    for k in range(TOP):
        named = ids_ref[k : k + 1, :] == expert
        value = jnp.sum(jnp.where(named, per_expert, 0.0), axis=0, keepdims=True)
        keep_ref[FEATS + k : FEATS + k + 1, :] = value
        send_ref[FEATS + k : FEATS + k + 1, :] = value


VMEM = pl.BlockSpec(memory_space=pltpu.VMEM)
SMEM = pl.BlockSpec(memory_space=pltpu.SMEM)


def per_device(tokens, out_grad, expert_ids, gate_values, w_gate, w_up, w_down):
    experts = lax.axis_size("ex")
    groups = lax.axis_size("grp")
    chips = groups // 2
    slots = experts * HALF
    count = tokens.shape[0]
    me = lax.axis_index("grp")
    core, z = me % 2, me // 2
    swap = [(i, i ^ 1) for i in range(groups)]
    up = [(i, (i + 2 - 4 * (i % 2)) % groups) for i in range(groups)]
    down = [(t, s) for s, t in up]
    core_arg = core.astype(jnp.int32).reshape(1)
    ids = expert_ids.T
    gates = gate_values.T

    own = jnp.stack([tokens.T, out_grad.T])
    peer = lax.ppermute(own, "grp", swap)
    rows, select = pl.pallas_call(
        dispatch_kernel,
        in_specs=[SMEM] + [VMEM] * 4,
        out_shape=(
            jax.ShapeDtypeStruct((slots, 2 * WIDE), BF16),
            jax.ShapeDtypeStruct((slots, count), BF16),
        ),
        scratch_shapes=[pltpu.VMEM((2 * WIDE, count), F32)],
        name="dispatch",
    )(core_arg, ids, gates, own, peer)

    own_w = pl.pallas_call(
        pack_kernel,
        out_shape=jax.ShapeDtypeStruct((chips, 3 * HID, WIDE), BF16),
        compiler_params=pltpu.CompilerParams(vmem_limit_bytes=32 * 1024 * 1024),
        name="pack",
    )(w_gate[0], w_up[0], w_down[0])
    peer_w = lax.ppermute(own_w, "grp", swap)

    rows = lax.all_to_all(
        rows.reshape(experts, HALF, 2 * WIDE), "ex", split_axis=0, concat_axis=0, tiled=True
    ).reshape(slots, 2 * WIDE)
    blocks, a, b = [rows], rows, rows
    for _ in range(3):
        a = lax.ppermute(a, "grp", up)
        b = lax.ppermute(b, "grp", down)
        blocks += [a, b]
    a = lax.ppermute(a[: slots // 2], "grp", up)
    b = lax.ppermute(b[slots // 2 :], "grp", down)
    turn = 1 - 2 * core
    order = jnp.stack(
        [(z + d * turn) % chips for d in (0, -1, 1, -2, 2, -3, 3, 4)]
    ).astype(jnp.int32)

    chunk = CHIP + 2
    pick = lambda i, order: (jnp.where(i < chips, order[jnp.minimum(i, chips - 1)], i - chips), 0, 0)
    whole = lambda s: pl.BlockSpec(s, lambda i, order: (0, 0))
    terms = pl.pallas_call(
        expert_kernel,
        grid_spec=pltpu.PrefetchScalarGridSpec(
            num_scalar_prefetch=1,
            grid=(2 * chips,),
            in_specs=[whole((slots, 2 * WIDE))] * 7
            + [whole((slots // 2, 2 * WIDE))] * 2
            + [pl.BlockSpec((1, 3 * HID, WIDE), pick)] * 2,
            out_specs=whole((chips * chunk, slots)),
            scratch_shapes=[
                pltpu.VMEM((3 * HID, slots), F32),
                pltpu.VMEM((3 * HID, slots), F32),
                pltpu.VMEM((2 * HID, slots), BF16),
                pltpu.VMEM((2 * HID, slots), BF16),
                pltpu.VMEM((chips * chunk, slots), F32),
            ],
        ),
        out_shape=jax.ShapeDtypeStruct((chips * chunk, slots), BF16),
        compiler_params=pltpu.CompilerParams(vmem_limit_bytes=32 * 1024 * 1024),
        name="expert",
    )(order, *blocks, a, b, own_w, peer_w)

    same_core = [list(range(c, groups, 2)) for c in range(2)]
    part = lax.psum_scatter(
        terms, "grp", scatter_dimension=0, axis_index_groups=same_core, tiled=True
    )
    ret = lax.all_to_all(
        part.T.reshape(experts, HALF, chunk), "ex", split_axis=0, concat_axis=0, tiled=True
    ).reshape(slots, chunk)
    keep, send = pl.pallas_call(
        combine_kernel,
        in_specs=[SMEM] + [VMEM] * 3,
        out_shape=(jax.ShapeDtypeStruct((FEATS + TOP, count), F32),) * 2,
        name="combine",
    )(core_arg, ret, select, ids)
    total = keep + lax.ppermute(send, "grp", swap)
    return total[:FEATS].astype(BF16).T, total[FEATS:].T


def solution(mesh):
    return jax.shard_map(
        per_device,
        mesh=mesh,
        in_specs=(
            P("ex", "grp"),
            P("ex", "grp"),
            P("ex", None),
            P("ex", None),
            P("ex", "grp", None),
            P("ex", "grp", None),
            P("ex", "grp", None),
        ),
        out_specs=(P("ex", "grp"), P("ex", None)),
        check_vma=False,
    )
```

```python
import functools

import jax
import jax.numpy as jnp
from jax import lax
from jax.experimental import pallas as pl
from jax.experimental.pallas import tpu as pltpu
from jax.sharding import PartitionSpec as P

TOP = 4
CAP = 16
HALF = CAP // 2
FEATS = 180
HIDDEN = 180
HID = 192
WIDE = 384
CHIP = 2 * FEATS
NT = (((1,), (1,)), ((), ()))
TN = (((0,), (0,)), ((), ()))
F32 = jnp.float32
BF16 = jnp.bfloat16


def iota(shape, dim):
    return lax.broadcasted_iota(jnp.int32, shape, dim)


def route_kernel(me_ref, ids_ref, gate_ref, sel_ref, weight_ref):
    slots, count = sel_ref.shape
    experts = slots // HALF
    gates = gate_ref[...].astype(F32)
    expert = iota((experts, count), 0)
    member = jnp.zeros((experts, count), F32)
    weight = jnp.zeros((experts, count), F32)
    for k in range(TOP):
        named = ids_ref[k : k + 1, :] == expert
        member = jnp.where(named, 1.0, member)
        weight = jnp.where(named, gates[k : k + 1, :], weight)
    earlier = jnp.where(iota((count, count), 0) < iota((count, count), 1), 1.0, 0.0)
    place = jnp.dot(member.astype(BF16), earlier.astype(BF16), preferred_element_type=F32)
    code = jnp.where(member > 0.0, place - (HALF * lax.rem(me_ref[0], 2)).astype(F32), -1.0)
    picked = code[:, None, :] == iota((experts, HALF, count), 1).astype(F32)
    sel_ref[...] = jnp.where(picked, 1.0, 0.0).reshape(slots, count).astype(BF16)
    weight_ref[...] = weight


def dispatch_kernel(me_ref, sel_ref, weight_ref, own_ref, peer_ref, rows_ref, feat_ref):
    slots, count = sel_ref.shape
    experts = slots // HALF
    core = lax.rem(me_ref[0], 2)
    select = sel_ref[...]
    spread = select.astype(F32).reshape(experts, HALF, count) * weight_ref[...][:, None, :]
    slot_weight = jnp.sum(spread.reshape(slots, count), axis=1, keepdims=True)
    feat_ref[...] = jnp.zeros_like(feat_ref)
    for part in range(2):
        own = own_ref[part].astype(F32)
        peer = peer_ref[part].astype(F32)
        base = part * WIDE
        feat_ref[base : base + FEATS, :] = jnp.where(core == 0, own, peer)
        feat_ref[base + FEATS : base + CHIP, :] = jnp.where(core == 0, peer, own)
    rows = lax.dot_general(
        select, feat_ref[...].astype(BF16), NT, preferred_element_type=F32
    )
    rows_ref[...] = jnp.where(iota(rows.shape, 1) == CHIP, slot_weight, rows).astype(BF16)


def pack_kernel(gate_ref, up_ref, down_ref, out_ref, source, packed, sems_in, sems_out):
    chips = packed.shape[0]
    loads = [
        pltpu.make_async_copy(ref, source.at[part], sems_in.at[part])
        for part, ref in enumerate((gate_ref, up_ref, down_ref))
    ]
    for load in loads:
        load.start()
    spare = HID - HIDDEN
    spot = iota((spare, WIDE), 1) == iota((spare, WIDE), 0) + CHIP
    mark = jnp.where(jnp.logical_and(spot, iota((spare, WIDE), 0) < 2), 1.0, 0.0)
    for part in range(3):
        loads[part].wait()
        for chip in range(chips):
            start = chip * CHIP
            low = start // 128 * 128
            high = min(low + 512, source.shape[2])
            w = source[part, :, low:high].astype(F32)
            w = w[:, start - low : start - low + CHIP]
            w = jnp.concatenate([w, jnp.zeros((HIDDEN, WIDE - CHIP), F32)], axis=1)
            tail = mark if part == 0 else jnp.zeros_like(mark)
            w = jnp.concatenate([w, tail], axis=0)
            packed[chip, part * HID : (part + 1) * HID, :] = w.astype(BF16)
    stores = [
        pltpu.make_async_copy(packed.at[chip], out_ref.at[chip], sems_out.at[chip])
        for chip in range(chips)
    ]
    for store in stores:
        store.start()
    for store in stores:
        store.wait()


def project(w, rows, total):
    fresh = (
        lax.dot_general(w[: 2 * HID, :], rows[:, :WIDE], NT, preferred_element_type=F32),
        lax.dot_general(w[2 * HID :, :], rows[:, WIDE:], NT, preferred_element_type=F32),
    )
    return fresh if total is None else (total[0] + fresh[0], total[1] + fresh[1])


def chip_of(me_ref, distance, chips):
    me = me_ref[0]
    return lax.rem(me // 2 + distance * (1 - 2 * lax.rem(me, 2)) + chips, chips)


def forward_kernel(places, me_ref, *refs):
    count = len(places)
    blocks, weights, sources, sums = refs[:count], refs[count : count + 2], refs[count + 2 : -2], refs[-2:]
    chips = weights[0].shape[0]
    totals = [(ref[: 2 * HID, :], ref[2 * HID :, :]) for ref in sources] or [None, None]
    for ref, place in zip(blocks, places):
        chip = chip_of(me_ref, place, chips)
        for i in range(2):
            totals[i] = project(weights[i][chip], ref[...], totals[i])
    for i in range(2):
        sums[i][: 2 * HID, :] = totals[i][0]
        sums[i][2 * HID :, :] = totals[i][1]


def backward_kernel(me_ref, rows_ref, own_w, peer_w, own_sum, peer_sum, out_ref, terms):
    weights = own_w, peer_w
    chips = own_w.shape[0]
    chip = chip_of(me_ref, chips // 2, chips)
    totals = [
        project(w_ref[chip], rows_ref[...], (sum_ref[: 2 * HID, :], sum_ref[2 * HID :, :]))
        for w_ref, sum_ref in zip(weights, (own_sum, peer_sum))
    ]
    grads, probs = [], []
    for pre, back in totals:
        pre_gate, pre_up = pre[:HID], pre[HID:]
        weight = pre_gate[HIDDEN : HIDDEN + 1] * (1.0 / chips)
        sig = jax.nn.sigmoid(pre_gate)
        act = pre_gate * sig
        live = iota(act.shape, 0) < HIDDEN
        probs.append(jnp.sum(jnp.where(live, back * (act * pre_up), 0.0), axis=0, keepdims=True))
        hid_grad = weight * back
        d_gate = hid_grad * pre_up * sig * (1.0 + pre_gate * (1.0 - sig))
        d_up = hid_grad * act
        grads.append([jnp.where(live, d_gate, 0.0), jnp.where(live, d_up, 0.0)])
    prob = probs[0] + probs[1]
    high = prob.astype(BF16).astype(F32)
    row = iota(grads[0][0].shape, 0)
    d_gate = jnp.where(row == HIDDEN, high, grads[0][0])
    grads[0][0] = jnp.where(row == HIDDEN + 1, prob - high, d_gate)
    grads = [jnp.concatenate(g, axis=0).astype(BF16) for g in grads]
    chunk = CHIP + 2
    for k in range(chips):
        value = None
        for i in range(2):
            term = lax.dot_general(
                weights[i][k, : 2 * HID, :], grads[i], TN, preferred_element_type=F32
            )
            value = term if value is None else value + term
        terms[k * chunk : (k + 1) * chunk, :] = value[:chunk, :]
    out_ref[...] = terms[...].astype(BF16)


def combine_kernel(me_ref, ret_ref, sel_ref, ids_ref, keep_ref, send_ref):
    slots, count = sel_ref.shape
    experts = slots // HALF
    core = lax.rem(me_ref[0], 2)
    ret = ret_ref[...]
    select = sel_ref[...]
    total = lax.dot_general(ret, select, TN, preferred_element_type=F32)
    first, second = total[:FEATS, :], total[FEATS:CHIP, :]
    keep_ref[:FEATS, :] = jnp.where(core == 0, first, second)
    send_ref[:FEATS, :] = jnp.where(core == 0, second, first)
    prob = ret[:, CHIP : CHIP + 1].astype(F32) + ret[:, CHIP + 1 : CHIP + 2].astype(F32)
    per_expert = jnp.sum((select.astype(F32) * prob).reshape(experts, HALF, count), axis=1)
    expert = iota((experts, count), 0)
    for k in range(TOP):
        named = ids_ref[k : k + 1, :] == expert
        value = jnp.sum(jnp.where(named, per_expert, 0.0), axis=0, keepdims=True)
        keep_ref[FEATS + k : FEATS + k + 1, :] = value
        send_ref[FEATS + k : FEATS + k + 1, :] = value


def finish_kernel(keep_ref, come_ref, tok_ref, gate_ref):
    total = keep_ref[...] + come_ref[...]
    tok_ref[...] = total[:FEATS, :].astype(BF16)
    gate_ref[...] = total[FEATS:, :]


VMEM = pl.BlockSpec(memory_space=pltpu.VMEM)
SMEM = pl.BlockSpec(memory_space=pltpu.SMEM)
HBM = pl.BlockSpec(memory_space=pltpu.HBM)
DMA = pltpu.SemaphoreType.DMA
SMALL = pltpu.CompilerParams(vmem_limit_bytes=16 * 1024 * 1024)
LARGE = pltpu.CompilerParams(vmem_limit_bytes=32 * 1024 * 1024)


def after(*values):
    return lax.optimization_barrier(values)


def per_device(tokens, out_grad, expert_ids, gate_values, w_gate, w_up, w_down):
    experts = lax.axis_size("ex")
    groups = lax.axis_size("grp")
    chips = groups // 2
    slots = experts * HALF
    count = tokens.shape[0]
    me = lax.axis_index("grp")
    swap = [(i, i ^ 1) for i in range(groups)]
    up = [(i, (i + 2 - 4 * (i % 2)) % groups) for i in range(groups)]
    cross = [(s ^ 1, t) for s, t in up]
    me_arg = me.astype(jnp.int32).reshape(1)
    ids = expert_ids.T
    gates = gate_values.T

    own = jnp.stack([tokens.T, out_grad.T])
    peer = lax.ppermute(own, "grp", swap)
    select, weight = pl.pallas_call(
        route_kernel,
        in_specs=[SMEM, VMEM, VMEM],
        out_shape=(
            jax.ShapeDtypeStruct((slots, count), BF16),
            jax.ShapeDtypeStruct((experts, count), F32),
        ),
        compiler_params=SMALL,
        name="route",
    )(me_arg, ids, gates)
    own_w = pl.pallas_call(
        pack_kernel,
        in_specs=[HBM] * 3,
        out_specs=HBM,
        out_shape=jax.ShapeDtypeStruct((chips, 3 * HID, WIDE), BF16),
        scratch_shapes=[
            pltpu.VMEM((3,) + w_gate.shape[1:], BF16),
            pltpu.VMEM((chips, 3 * HID, WIDE), BF16),
            DMA((3,)),
            DMA((chips,)),
        ],
        compiler_params=pltpu.CompilerParams(vmem_limit_bytes=60 * 1024 * 1024),
        name="pack",
    )(w_gate[0], w_up[0], w_down[0])
    peer, own_w = after(peer, own_w)
    peer_w = lax.ppermute(own_w, "grp", swap)
    rows = pl.pallas_call(
        dispatch_kernel,
        in_specs=[SMEM] + [VMEM] * 4,
        out_shape=jax.ShapeDtypeStruct((slots, 2 * WIDE), BF16),
        scratch_shapes=[pltpu.VMEM((2 * WIDE, count), F32)],
        compiler_params=SMALL,
        name="dispatch",
    )(me_arg, select, weight, own, peer)
    rows = lax.all_to_all(
        rows.reshape(experts, HALF, 2 * WIDE), "ex", split_axis=0, concat_axis=0, tiled=True
    ).reshape(slots, 2 * WIDE)

    mine1 = lax.ppermute(rows, "grp", up)
    other1 = lax.ppermute(rows, "grp", cross)
    mine2 = lax.ppermute(mine1, "grp", up)
    other2 = lax.ppermute(other1, "grp", up)
    came1 = lax.ppermute(other1, "grp", swap)
    mine3 = lax.ppermute(mine2, "grp", up)
    other2, came1 = after(other2, came1)
    other3 = lax.ppermute(other2, "grp", up)
    mine4 = lax.ppermute(mine3, "grp", up)
    came2 = lax.ppermute(other2, "grp", swap)
    came3 = lax.ppermute(other3, "grp", swap)

    def forward(blocks, places, sums):
        n = len(blocks)
        return pl.pallas_call(
            functools.partial(forward_kernel, places),
            in_specs=[SMEM] + [VMEM] * (n + 2 + len(sums)),
            out_specs=[VMEM] * 2,
            out_shape=[jax.ShapeDtypeStruct((3 * HID, slots), F32)] * 2,
            compiler_params=LARGE,
            cost_estimate=pl.CostEstimate(
                flops=n * 4 * slots * 3 * HID * WIDE,
                bytes_accessed=n * (slots + 3 * HID) * 4 * WIDE + 8 * 3 * HID * slots,
                transcendentals=0,
            ),
            name="forward",
        )(me_arg, *blocks, own_w, peer_w, *sums)

    sums = forward([rows, mine1, came1, mine2, came2], (0, -1, 1, -2, 2), ())
    sums = forward([mine3, came3], (-3, 3), sums)
    chunk = CHIP + 2
    terms = pl.pallas_call(
        backward_kernel,
        in_specs=[SMEM] + [VMEM] * 5,
        out_specs=VMEM,
        out_shape=jax.ShapeDtypeStruct((chips * chunk, slots), BF16),
        scratch_shapes=[pltpu.VMEM((chips * chunk, slots), F32)],
        compiler_params=LARGE,
        name="backward",
    )(me_arg, mine4, own_w, peer_w, *sums)

    same_core = [list(range(c, groups, 2)) for c in range(2)]
    part = lax.psum_scatter(
        terms, "grp", scatter_dimension=0, axis_index_groups=same_core, tiled=True
    )
    ret = lax.all_to_all(
        part.T.reshape(experts, HALF, chunk), "ex", split_axis=0, concat_axis=0, tiled=True
    ).reshape(slots, chunk)
    keep, send = pl.pallas_call(
        combine_kernel,
        in_specs=[SMEM] + [VMEM] * 3,
        out_shape=(jax.ShapeDtypeStruct((FEATS + TOP, count), F32),) * 2,
        compiler_params=SMALL,
        name="combine",
    )(me_arg, ret, select, ids)
    tok, gate = pl.pallas_call(
        finish_kernel,
        out_shape=(
            jax.ShapeDtypeStruct((FEATS, count), BF16),
            jax.ShapeDtypeStruct((TOP, count), F32),
        ),
        compiler_params=SMALL,
        name="finish",
    )(keep, lax.ppermute(send, "grp", swap))
    return tok.T, gate.T


def solution(mesh):
    return jax.shard_map(
        per_device,
        mesh=mesh,
        in_specs=(
            P("ex", "grp"),
            P("ex", "grp"),
            P("ex", None),
            P("ex", None),
            P("ex", "grp", None),
            P("ex", "grp", None),
            P("ex", "grp", None),
        ),
        out_specs=(P("ex", "grp"), P("ex", None)),
        check_vma=False,
    )
```

```python
import functools

import jax
import jax.numpy as jnp
from jax import lax
from jax.experimental import pallas as pl
from jax.experimental.pallas import tpu as pltpu
from jax.sharding import PartitionSpec as P

TOP = 4
CAP = 16
HALF = CAP // 2
FEATS = 180
HIDDEN = 180
HID = 192
WIDE = 384
CHIP = 2 * FEATS
BACK = FEATS + 2
NT = (((1,), (1,)), ((), ()))
TN = (((0,), (0,)), ((), ()))
F32 = jnp.float32
BF16 = jnp.bfloat16


def iota(shape, dim):
    return lax.broadcasted_iota(jnp.int32, shape, dim)


def dispatch_kernel(ids_ref, gate_ref, tok_ref, grad_ref, rows_ref, sel_ref, feat_ref):
    slots, count = sel_ref.shape
    half = slots // 2
    experts = half // HALF
    gates = gate_ref[...].astype(F32)
    expert = iota((experts, count), 0)
    member = jnp.zeros((experts, count), F32)
    weight = jnp.zeros((experts, count), F32)
    for k in range(TOP):
        named = ids_ref[k : k + 1, :] == expert
        member = jnp.where(named, 1.0, member)
        weight = jnp.where(named, gates[k : k + 1, :], weight)
    earlier = jnp.where(iota((count, count), 0) < iota((count, count), 1), 1.0, 0.0)
    place = jnp.dot(member.astype(BF16), earlier.astype(BF16), preferred_element_type=F32)
    code = jnp.where(member > 0.0, place, -1.0)
    feat_ref[...] = jnp.zeros_like(feat_ref)
    feat_ref[:FEATS, :] = tok_ref[...].astype(F32)
    feat_ref[FEATS:CHIP, :] = grad_ref[...].astype(F32)
    feats = feat_ref[...].astype(BF16)
    for core in range(2):
        slot = iota((experts, HALF, count), 1).astype(F32) + float(HALF * core)
        picked = code[:, None, :] == slot
        select = jnp.where(picked, 1.0, 0.0).reshape(half, count).astype(BF16)
        slot_weight = jnp.sum(
            jnp.where(picked, weight[:, None, :], 0.0).reshape(half, count), axis=1, keepdims=True
        )
        rows = lax.dot_general(select, feats, NT, preferred_element_type=F32)
        rows = jnp.where(iota(rows.shape, 1) == CHIP, slot_weight, rows)
        sel_ref[core * half : (core + 1) * half, :] = select
        rows_ref[core * half : (core + 1) * half, :] = rows.astype(BF16)


def join_kernel(parts_ref, rows_ref):
    first, second = parts_ref[0].astype(F32), parts_ref[1].astype(F32)
    rest = first[:, CHIP:WIDE]
    tok = jnp.concatenate([first[:, :FEATS], second[:, :FEATS], rest], axis=1)
    grad = jnp.concatenate([first[:, FEATS:CHIP], second[:, FEATS:CHIP], rest], axis=1)
    rows_ref[:, :WIDE] = tok.astype(BF16)
    rows_ref[:, WIDE:] = grad.astype(BF16)


def pack_kernel(gate_ref, up_ref, down_ref, out_ref, source, packed, sems_in, sems_out):
    chips = packed.shape[0]
    loads = [
        pltpu.make_async_copy(ref, source.at[part], sems_in.at[part])
        for part, ref in enumerate((gate_ref, up_ref, down_ref))
    ]
    for load in loads:
        load.start()
    spare = HID - HIDDEN
    spot = iota((spare, WIDE), 1) == iota((spare, WIDE), 0) + CHIP
    mark = jnp.where(jnp.logical_and(spot, iota((spare, WIDE), 0) < 2), 1.0, 0.0)
    stores = []
    for part in range(3):
        loads[part].wait()
        for chip in range(chips):
            start = chip * CHIP
            low = start // 128 * 128
            high = min(low + 512, source.shape[2])
            w = source[part, :, low:high].astype(F32)
            w = w[:, start - low : start - low + CHIP]
            w = jnp.concatenate([w, jnp.zeros((HIDDEN, WIDE - CHIP), F32)], axis=1)
            tail = mark if part == 0 else jnp.zeros_like(mark)
            w = jnp.concatenate([w, tail], axis=0)
            packed[chip, part * HID : (part + 1) * HID, :] = w.astype(BF16)
        rows = pl.ds(part * HID, HID)
        stores.append(
            pltpu.make_async_copy(
                packed.at[:, rows, :], out_ref.at[:, rows, :], sems_out.at[part]
            )
        )
        stores[part].start()
    for store in stores:
        store.wait()


def project(w, rows, total):
    fresh = (
        lax.dot_general(w[: 2 * HID, :], rows[:, :WIDE], NT, preferred_element_type=F32),
        lax.dot_general(w[2 * HID :, :], rows[:, WIDE:], NT, preferred_element_type=F32),
    )
    return fresh if total is None else (total[0] + fresh[0], total[1] + fresh[1])


def chip_of(me_ref, distance, chips):
    me = me_ref[0]
    return lax.rem(me // 2 + distance * (1 - 2 * lax.rem(me, 2)) + chips, chips)


def forward_kernel(places, me_ref, *refs):
    count = len(places)
    blocks, weights, sources, sums = refs[:count], refs[count : count + 2], refs[count + 2 : -2], refs[-2:]
    chips = weights[0].shape[0]
    totals = [(ref[: 2 * HID, :], ref[2 * HID :, :]) for ref in sources] or [None, None]
    for ref, place in zip(blocks, places):
        chip = chip_of(me_ref, place, chips)
        for i in range(2):
            totals[i] = project(weights[i][chip], ref[...], totals[i])
    for i in range(2):
        sums[i][: 2 * HID, :] = totals[i][0]
        sums[i][2 * HID :, :] = totals[i][1]


def backward_kernel(me_ref, rows_ref, own_w, peer_w, own_sum, peer_sum, out_ref, terms):
    weights = own_w, peer_w
    chips = own_w.shape[0]
    chip = chip_of(me_ref, chips // 2, chips)
    totals = [
        project(w_ref[chip], rows_ref[...], (sum_ref[: 2 * HID, :], sum_ref[2 * HID :, :]))
        for w_ref, sum_ref in zip(weights, (own_sum, peer_sum))
    ]
    grads, probs = [], []
    for pre, back in totals:
        pre_gate, pre_up = pre[:HID], pre[HID:]
        weight = pre_gate[HIDDEN : HIDDEN + 1] * (1.0 / chips)
        sig = jax.nn.sigmoid(pre_gate)
        act = pre_gate * sig
        live = iota(act.shape, 0) < HIDDEN
        probs.append(jnp.sum(jnp.where(live, back * (act * pre_up), 0.0), axis=0, keepdims=True))
        hid_grad = weight * back
        d_gate = hid_grad * pre_up * sig * (1.0 + pre_gate * (1.0 - sig))
        d_up = hid_grad * act
        grads.append([jnp.where(live, d_gate, 0.0), jnp.where(live, d_up, 0.0)])
    prob = probs[0] + probs[1]
    high = prob.astype(BF16).astype(F32)
    row = iota(grads[0][0].shape, 0)
    d_gate = jnp.where(row == HIDDEN, high, grads[0][0])
    grads[0][0] = jnp.where(row == HIDDEN + 1, prob - high, d_gate)
    grads = [jnp.concatenate(g, axis=0).astype(BF16) for g in grads]
    for k in range(chips):
        value = None
        for i in range(2):
            term = lax.dot_general(
                weights[i][k, : 2 * HID, :], grads[i], TN, preferred_element_type=F32
            )
            value = term if value is None else value + term
        for part in range(2):
            start = (2 * k + part) * BACK
            terms[start : start + FEATS, :] = value[part * FEATS : (part + 1) * FEATS, :]
            terms[start + FEATS : start + BACK, :] = value[CHIP : CHIP + 2, :]
    out_ref[...] = terms[...].astype(BF16)


def combine_kernel(ret_ref, sel_ref, ids_ref, tok_ref, gate_ref):
    slots, count = sel_ref.shape
    experts = slots // CAP
    ret = ret_ref[...]
    select = sel_ref[...]
    total = lax.dot_general(ret, select, TN, preferred_element_type=F32)
    tok_ref[...] = total[:FEATS, :].astype(BF16)
    prob = ret[:, FEATS : FEATS + 1].astype(F32) + ret[:, FEATS + 1 : FEATS + 2].astype(F32)
    spread = (select.astype(F32) * prob).reshape(2, experts, HALF, count)
    per_expert = jnp.sum(spread[0] + spread[1], axis=1)
    expert = iota((experts, count), 0)
    for k in range(TOP):
        named = ids_ref[k : k + 1, :] == expert
        gate_ref[k : k + 1, :] = jnp.sum(
            jnp.where(named, per_expert, 0.0), axis=0, keepdims=True
        )


VMEM = pl.BlockSpec(memory_space=pltpu.VMEM)
SMEM = pl.BlockSpec(memory_space=pltpu.SMEM)
HBM = pl.BlockSpec(memory_space=pltpu.HBM)
DMA = pltpu.SemaphoreType.DMA
SMALL = pltpu.CompilerParams(vmem_limit_bytes=16 * 1024 * 1024)
LARGE = pltpu.CompilerParams(vmem_limit_bytes=32 * 1024 * 1024)


def after(*values):
    return lax.optimization_barrier(values)


def per_device(tokens, out_grad, expert_ids, gate_values, w_gate, w_up, w_down):
    experts = lax.axis_size("ex")
    groups = lax.axis_size("grp")
    chips = groups // 2
    slots = experts * HALF
    count = tokens.shape[0]
    me_arg = lax.axis_index("grp").astype(jnp.int32).reshape(1)
    swap = [(i, i ^ 1) for i in range(groups)]
    up = [(i, (i + 2 - 4 * (i % 2)) % groups) for i in range(groups)]
    cross = [(s ^ 1, t) for s, t in up]
    both_cores = [list(range(2 * z * experts, 2 * (z + 1) * experts)) for z in range(chips)]
    ids, me_arg = after(expert_ids.T, me_arg)

    def exchange(rows):
        return lax.all_to_all(
            rows.reshape(2 * experts, HALF, rows.shape[-1]),
            ("grp", "ex"),
            split_axis=0,
            concat_axis=0,
            axis_index_groups=both_cores,
            tiled=True,
        )

    rows, select = pl.pallas_call(
        dispatch_kernel,
        in_specs=[VMEM] * 4,
        out_shape=(
            jax.ShapeDtypeStruct((2 * slots, WIDE), BF16),
            jax.ShapeDtypeStruct((2 * slots, count), BF16),
        ),
        scratch_shapes=[pltpu.VMEM((WIDE, count), F32)],
        compiler_params=SMALL,
        name="dispatch",
    )(ids, gate_values.T, tokens.T, out_grad.T)
    own_w = pl.pallas_call(
        pack_kernel,
        in_specs=[HBM] * 3,
        out_specs=HBM,
        out_shape=jax.ShapeDtypeStruct((chips, 3 * HID, WIDE), BF16),
        scratch_shapes=[
            pltpu.VMEM((3,) + w_gate.shape[1:], BF16),
            pltpu.VMEM((chips, 3 * HID, WIDE), BF16),
            DMA((3,)),
            DMA((3,)),
        ],
        compiler_params=pltpu.CompilerParams(vmem_limit_bytes=60 * 1024 * 1024),
        name="pack",
    )(w_gate[0], w_up[0], w_down[0])
    rows, own_w = after(rows, own_w)
    rows = pl.pallas_call(
        join_kernel,
        in_specs=[VMEM],
        out_specs=VMEM,
        out_shape=jax.ShapeDtypeStruct((slots, 2 * WIDE), BF16),
        compiler_params=SMALL,
        name="join",
    )(exchange(rows).reshape(2, slots, WIDE))

    rows, own_w = after(rows, own_w)
    peer_w = lax.ppermute(own_w, "grp", swap)
    mine1 = lax.ppermute(rows, "grp", up)
    other1 = lax.ppermute(rows, "grp", cross)
    mine2 = lax.ppermute(mine1, "grp", up)
    other2 = lax.ppermute(other1, "grp", up)
    other1, mine2 = after(other1, mine2)
    came1 = lax.ppermute(other1, "grp", swap)
    mine3 = lax.ppermute(mine2, "grp", up)
    other3 = lax.ppermute(other2, "grp", up)
    mine3, came1 = after(mine3, came1)
    mine4 = lax.ppermute(mine3, "grp", up)
    other2, other3 = after(other2, other3)
    came2 = lax.ppermute(other2, "grp", swap)
    came3 = lax.ppermute(other3, "grp", swap)

    def forward(blocks, places, sums):
        n = len(blocks)
        return pl.pallas_call(
            functools.partial(forward_kernel, places),
            in_specs=[SMEM] + [VMEM] * (n + 2 + len(sums)),
            out_specs=[VMEM] * 2,
            out_shape=[jax.ShapeDtypeStruct((3 * HID, slots), F32)] * 2,
            compiler_params=LARGE,
            cost_estimate=pl.CostEstimate(
                flops=n * 4 * slots * 3 * HID * WIDE,
                bytes_accessed=n * (slots + 3 * HID) * 4 * WIDE + 8 * 3 * HID * slots,
                transcendentals=0,
            ),
            name="forward",
        )(me_arg, *blocks, own_w, peer_w, *sums)

    sums = forward([rows, mine1, came1, mine2, came2], (0, -1, 1, -2, 2), ())
    sums = forward([mine3, came3], (-3, 3), sums)
    terms = pl.pallas_call(
        backward_kernel,
        in_specs=[SMEM] + [VMEM] * 5,
        out_specs=VMEM,
        out_shape=jax.ShapeDtypeStruct((groups * BACK, slots), BF16),
        scratch_shapes=[pltpu.VMEM((groups * BACK, slots), F32)],
        compiler_params=LARGE,
        name="backward",
    )(me_arg, mine4, own_w, peer_w, *sums)

    same_core = [list(range(c, groups, 2)) for c in range(2)]
    part = lax.psum_scatter(
        terms, "grp", scatter_dimension=0, axis_index_groups=same_core, tiled=True
    )
    ret = exchange(part.reshape(2, BACK, slots).transpose(0, 2, 1)).reshape(2 * slots, BACK)
    tok, gate = pl.pallas_call(
        combine_kernel,
        in_specs=[VMEM] * 3,
        out_shape=(
            jax.ShapeDtypeStruct((FEATS, count), BF16),
            jax.ShapeDtypeStruct((TOP, count), F32),
        ),
        compiler_params=SMALL,
        name="combine",
    )(ret, select, ids)
    return tok.T, gate.T


def solution(mesh):
    return jax.shard_map(
        per_device,
        mesh=mesh,
        in_specs=(
            P("ex", "grp"),
            P("ex", "grp"),
            P("ex", None),
            P("ex", None),
            P("ex", "grp", None),
            P("ex", "grp", None),
            P("ex", "grp", None),
        ),
        out_specs=(P("ex", "grp"), P("ex", None)),
        check_vma=False,
    )
```

```python
import functools

import jax
import jax.numpy as jnp
from jax import lax
from jax.experimental import pallas as pl
from jax.experimental.pallas import tpu as pltpu
from jax.sharding import PartitionSpec as P

TOP = 4
CAP = 16
HALF = CAP // 2
FEATS = 180
HIDDEN = 180
HID = 192
WIDE = 384
CHIP = 2 * FEATS
BACK = FEATS + 2
NT = (((1,), (1,)), ((), ()))
TN = (((0,), (0,)), ((), ()))
F32 = jnp.float32
BF16 = jnp.bfloat16


def iota(shape, dim):
    return lax.broadcasted_iota(jnp.int32, shape, dim)


def dispatch_kernel(ids_ref, gate_ref, tok_ref, grad_ref, rows_ref, sel_ref, feat_ref):
    slots, count = sel_ref.shape
    half = slots // 2
    experts = half // HALF
    gates = gate_ref[...].astype(F32)
    expert = iota((experts, count), 0)
    member = jnp.zeros((experts, count), F32)
    weight = jnp.zeros((experts, count), F32)
    for k in range(TOP):
        named = ids_ref[k : k + 1, :] == expert
        member = jnp.where(named, 1.0, member)
        weight = jnp.where(named, gates[k : k + 1, :], weight)
    earlier = jnp.where(iota((count, count), 0) < iota((count, count), 1), 1.0, 0.0)
    place = jnp.dot(member.astype(BF16), earlier.astype(BF16), preferred_element_type=F32)
    code = jnp.where(member > 0.0, place, -1.0)
    feat_ref[...] = jnp.zeros_like(feat_ref)
    feat_ref[:FEATS, :] = tok_ref[...].astype(F32)
    feat_ref[FEATS:CHIP, :] = grad_ref[...].astype(F32)
    feats = feat_ref[...].astype(BF16)
    for core in range(2):
        slot = iota((experts, HALF, count), 1).astype(F32) + float(HALF * core)
        picked = code[:, None, :] == slot
        select = jnp.where(picked, 1.0, 0.0).reshape(half, count).astype(BF16)
        slot_weight = jnp.sum(
            jnp.where(picked, weight[:, None, :], 0.0).reshape(half, count), axis=1, keepdims=True
        )
        rows = lax.dot_general(select, feats, NT, preferred_element_type=F32)
        rows = jnp.where(iota(rows.shape, 1) == CHIP, slot_weight, rows)
        sel_ref[core * half : (core + 1) * half, :] = select
        rows_ref[core * half : (core + 1) * half, :] = rows.astype(BF16)


def join_kernel(parts_ref, rows_ref):
    first, second = parts_ref[0].astype(F32), parts_ref[1].astype(F32)
    rest = first[:, CHIP:WIDE]
    tok = jnp.concatenate([first[:, :FEATS], second[:, :FEATS], rest], axis=1)
    grad = jnp.concatenate([first[:, FEATS:CHIP], second[:, FEATS:CHIP], rest], axis=1)
    rows_ref[:, :WIDE] = tok.astype(BF16)
    rows_ref[:, WIDE:] = grad.astype(BF16)


def pack_kernel(gate_ref, up_ref, down_ref, out_ref, source, packed, sems_in, sems_out):
    chips = packed.shape[0]
    loads = [
        pltpu.make_async_copy(ref, source.at[part], sems_in.at[part])
        for part, ref in enumerate((gate_ref, up_ref, down_ref))
    ]
    for load in loads:
        load.start()
    spare = HID - HIDDEN
    spot = iota((spare, WIDE), 1) == iota((spare, WIDE), 0) + CHIP
    mark = jnp.where(jnp.logical_and(spot, iota((spare, WIDE), 0) < 2), 1.0, 0.0)
    stores = []
    for part in range(3):
        loads[part].wait()
        for chip in range(chips):
            start = chip * CHIP
            low = start // 128 * 128
            high = min(low + 512, source.shape[2])
            w = source[part, :, low:high].astype(F32)
            w = w[:, start - low : start - low + CHIP]
            w = jnp.concatenate([w, jnp.zeros((HIDDEN, WIDE - CHIP), F32)], axis=1)
            tail = mark if part == 0 else jnp.zeros_like(mark)
            w = jnp.concatenate([w, tail], axis=0)
            packed[chip, part * HID : (part + 1) * HID, :] = w.astype(BF16)
        rows = pl.ds(part * HID, HID)
        stores.append(
            pltpu.make_async_copy(
                packed.at[:, rows, :], out_ref.at[:, rows, :], sems_out.at[part]
            )
        )
        stores[part].start()
    for store in stores:
        store.wait()


def project(w, rows, total):
    fresh = (
        lax.dot_general(w[: 2 * HID, :], rows[:, :WIDE], NT, preferred_element_type=F32),
        lax.dot_general(w[2 * HID :, :], rows[:, WIDE:], NT, preferred_element_type=F32),
    )
    return fresh if total is None else (total[0] + fresh[0], total[1] + fresh[1])


def chip_of(me_ref, distance, chips):
    me = me_ref[0]
    return lax.rem(me // 2 + distance * (1 - 2 * lax.rem(me, 2)) + chips, chips)


def forward_kernel(places, me_ref, *refs):
    count = len(places)
    blocks, weights, sources, sums = refs[:count], refs[count : count + 2], refs[count + 2 : -2], refs[-2:]
    chips = weights[0].shape[0]
    totals = [(ref[: 2 * HID, :], ref[2 * HID :, :]) for ref in sources] or [None, None]
    for ref, place in zip(blocks, places):
        chip = chip_of(me_ref, place, chips)
        for i in range(2):
            totals[i] = project(weights[i][chip], ref[...], totals[i])
    for i in range(2):
        sums[i][: 2 * HID, :] = totals[i][0]
        sums[i][2 * HID :, :] = totals[i][1]


def backward_kernel(own_w, peer_w, own_sum, peer_sum, out_ref, terms):
    weights = own_w, peer_w
    chips = own_w.shape[0]
    totals = [(ref[: 2 * HID, :], ref[2 * HID :, :]) for ref in (own_sum, peer_sum)]
    grads, probs = [], []
    for pre, back in totals:
        pre_gate, pre_up = pre[:HID], pre[HID:]
        weight = pre_gate[HIDDEN : HIDDEN + 1] * (1.0 / chips)
        sig = jax.nn.sigmoid(pre_gate)
        act = pre_gate * sig
        live = iota(act.shape, 0) < HIDDEN
        probs.append(jnp.sum(jnp.where(live, back * (act * pre_up), 0.0), axis=0, keepdims=True))
        hid_grad = weight * back
        d_gate = hid_grad * pre_up * sig * (1.0 + pre_gate * (1.0 - sig))
        d_up = hid_grad * act
        grads.append([jnp.where(live, d_gate, 0.0), jnp.where(live, d_up, 0.0)])
    prob = probs[0] + probs[1]
    high = prob.astype(BF16).astype(F32)
    row = iota(grads[0][0].shape, 0)
    d_gate = jnp.where(row == HIDDEN, high, grads[0][0])
    grads[0][0] = jnp.where(row == HIDDEN + 1, prob - high, d_gate)
    grads = [jnp.concatenate(g, axis=0).astype(BF16) for g in grads]
    for k in range(chips):
        value = None
        for i in range(2):
            term = lax.dot_general(
                weights[i][k, : 2 * HID, :], grads[i], TN, preferred_element_type=F32
            )
            value = term if value is None else value + term
        for part in range(2):
            start = (2 * k + part) * BACK
            terms[start : start + FEATS, :] = value[part * FEATS : (part + 1) * FEATS, :]
            terms[start + FEATS : start + BACK, :] = value[CHIP : CHIP + 2, :]
    out_ref[...] = terms[...].astype(BF16)


def combine_kernel(ret_ref, sel_ref, ids_ref, tok_ref, gate_ref):
    slots, count = sel_ref.shape
    experts = slots // CAP
    ret = ret_ref[...]
    select = sel_ref[...]
    total = lax.dot_general(ret, select, TN, preferred_element_type=F32)
    tok_ref[...] = total[:FEATS, :].astype(BF16)
    prob = ret[:, FEATS : FEATS + 1].astype(F32) + ret[:, FEATS + 1 : FEATS + 2].astype(F32)
    spread = (select.astype(F32) * prob).reshape(2, experts, HALF, count)
    per_expert = jnp.sum(spread[0] + spread[1], axis=1)
    expert = iota((experts, count), 0)
    for k in range(TOP):
        named = ids_ref[k : k + 1, :] == expert
        gate_ref[k : k + 1, :] = jnp.sum(
            jnp.where(named, per_expert, 0.0), axis=0, keepdims=True
        )


VMEM = pl.BlockSpec(memory_space=pltpu.VMEM)
SMEM = pl.BlockSpec(memory_space=pltpu.SMEM)
HBM = pl.BlockSpec(memory_space=pltpu.HBM)
DMA = pltpu.SemaphoreType.DMA
SMALL = pltpu.CompilerParams(vmem_limit_bytes=16 * 1024 * 1024)
LARGE = pltpu.CompilerParams(vmem_limit_bytes=32 * 1024 * 1024)


def after(*values):
    return lax.optimization_barrier(values)


def per_device(tokens, out_grad, expert_ids, gate_values, w_gate, w_up, w_down):
    experts = lax.axis_size("ex")
    groups = lax.axis_size("grp")
    chips = groups // 2
    slots = experts * HALF
    count = tokens.shape[0]
    me_arg = lax.axis_index("grp").astype(jnp.int32).reshape(1)
    swap = [(i, i ^ 1) for i in range(groups)]
    up = [(i, (i + 2 - 4 * (i % 2)) % groups) for i in range(groups)]
    cross = [(s ^ 1, t) for s, t in up]
    leave = [(s, t ^ 1) for s, t in up]
    both_cores = [list(range(2 * z * experts, 2 * (z + 1) * experts)) for z in range(chips)]
    ids, me_arg = after(expert_ids.T, me_arg)

    def exchange(rows):
        return lax.all_to_all(
            rows.reshape(2 * experts, HALF, rows.shape[-1]),
            ("grp", "ex"),
            split_axis=0,
            concat_axis=0,
            axis_index_groups=both_cores,
            tiled=True,
        )

    rows, select = pl.pallas_call(
        dispatch_kernel,
        in_specs=[VMEM] * 4,
        out_shape=(
            jax.ShapeDtypeStruct((2 * slots, WIDE), BF16),
            jax.ShapeDtypeStruct((2 * slots, count), BF16),
        ),
        scratch_shapes=[pltpu.VMEM((WIDE, count), F32)],
        compiler_params=SMALL,
        name="dispatch",
    )(ids, gate_values.T, tokens.T, out_grad.T)
    own_w = pl.pallas_call(
        pack_kernel,
        in_specs=[HBM] * 3,
        out_specs=HBM,
        out_shape=jax.ShapeDtypeStruct((chips, 3 * HID, WIDE), BF16),
        scratch_shapes=[
            pltpu.VMEM((3,) + w_gate.shape[1:], BF16),
            pltpu.VMEM((chips, 3 * HID, WIDE), BF16),
            DMA((3,)),
            DMA((3,)),
        ],
        compiler_params=pltpu.CompilerParams(vmem_limit_bytes=60 * 1024 * 1024),
        name="pack",
    )(w_gate[0], w_up[0], w_down[0])
    rows, own_w = after(rows, own_w)
    rows = pl.pallas_call(
        join_kernel,
        in_specs=[VMEM],
        out_specs=VMEM,
        out_shape=jax.ShapeDtypeStruct((slots, 2 * WIDE), BF16),
        compiler_params=SMALL,
        name="join",
    )(exchange(rows).reshape(2, slots, WIDE))

    rows, own_w = after(rows, own_w)
    peer_w = lax.ppermute(own_w, "grp", swap)
    mine1 = lax.ppermute(rows, "grp", up)
    other1 = lax.ppermute(rows, "grp", cross)
    mine2 = lax.ppermute(mine1, "grp", up)
    other2 = lax.ppermute(other1, "grp", up)
    other1, mine2 = after(other1, mine2)
    came1 = lax.ppermute(other1, "grp", swap)
    mine3 = lax.ppermute(mine2, "grp", up)
    other3 = lax.ppermute(other2, "grp", up)
    came4 = lax.ppermute(other3, "grp", leave)
    other2, other3 = after(other2, other3)
    came2 = lax.ppermute(other2, "grp", swap)
    came3 = lax.ppermute(other3, "grp", swap)

    def forward(blocks, places, sums):
        n = len(blocks)
        return pl.pallas_call(
            functools.partial(forward_kernel, places),
            in_specs=[SMEM] + [VMEM] * (n + 2 + len(sums)),
            out_specs=[VMEM] * 2,
            out_shape=[jax.ShapeDtypeStruct((3 * HID, slots), F32)] * 2,
            compiler_params=LARGE,
            cost_estimate=pl.CostEstimate(
                flops=n * 4 * slots * 3 * HID * WIDE,
                bytes_accessed=n * (slots + 3 * HID) * 4 * WIDE + 8 * 3 * HID * slots,
                transcendentals=0,
            ),
            name="forward",
        )(me_arg, *blocks, own_w, peer_w, *sums)

    sums = forward([rows, mine1, mine2, came1], (0, -1, -2, 1), ())
    sums = forward([mine3, came4], (-3, 4), sums)
    sums = forward([came2, came3], (2, 3), sums)
    terms = pl.pallas_call(
        backward_kernel,
        in_specs=[VMEM] * 4,
        out_specs=VMEM,
        out_shape=jax.ShapeDtypeStruct((groups * BACK, slots), BF16),
        scratch_shapes=[pltpu.VMEM((groups * BACK, slots), F32)],
        compiler_params=LARGE,
        name="backward",
    )(own_w, peer_w, *sums)

    same_core = [list(range(c, groups, 2)) for c in range(2)]
    part = lax.psum_scatter(
        terms, "grp", scatter_dimension=0, axis_index_groups=same_core, tiled=True
    )
    ret = exchange(part.reshape(2, BACK, slots).transpose(0, 2, 1)).reshape(2 * slots, BACK)
    tok, gate = pl.pallas_call(
        combine_kernel,
        in_specs=[VMEM] * 3,
        out_shape=(
            jax.ShapeDtypeStruct((FEATS, count), BF16),
            jax.ShapeDtypeStruct((TOP, count), F32),
        ),
        compiler_params=SMALL,
        name="combine",
    )(ret, select, ids)
    return tok.T, gate.T


def solution(mesh):
    return jax.shard_map(
        per_device,
        mesh=mesh,
        in_specs=(
            P("ex", "grp"),
            P("ex", "grp"),
            P("ex", None),
            P("ex", None),
            P("ex", "grp", None),
            P("ex", "grp", None),
            P("ex", "grp", None),
        ),
        out_specs=(P("ex", "grp"), P("ex", None)),
        check_vma=False,
    )
```

```python
import functools

import jax
import jax.numpy as jnp
from jax import lax
from jax.experimental import pallas as pl
from jax.experimental.pallas import tpu as pltpu
from jax.sharding import PartitionSpec as P

TOP = 4
CAP = 16
HALF = CAP // 2
FEATS = 180
HIDDEN = 180
HID = 192
WIDE = 384
CHIP = 2 * FEATS
BACK = FEATS + 2
NT = (((1,), (1,)), ((), ()))
TN = (((0,), (0,)), ((), ()))
F32 = jnp.float32
BF16 = jnp.bfloat16


def iota(shape, dim):
    return lax.broadcasted_iota(jnp.int32, shape, dim)


def dispatch_kernel(ids_ref, gate_ref, tok_ref, grad_ref, rows_ref, sel_ref, feat_ref):
    slots, count = sel_ref.shape
    half = slots // 2
    experts = half // HALF
    gates = gate_ref[...].astype(F32)
    expert = iota((experts, count), 0)
    member = jnp.zeros((experts, count), F32)
    weight = jnp.zeros((experts, count), F32)
    for k in range(TOP):
        named = ids_ref[k : k + 1, :] == expert
        member = jnp.where(named, 1.0, member)
        weight = jnp.where(named, gates[k : k + 1, :], weight)
    earlier = jnp.where(iota((count, count), 0) < iota((count, count), 1), 1.0, 0.0)
    place = jnp.dot(member.astype(BF16), earlier.astype(BF16), preferred_element_type=F32)
    code = jnp.where(member > 0.0, place, -1.0)
    feat_ref[...] = jnp.zeros_like(feat_ref)
    feat_ref[:FEATS, :] = tok_ref[...].astype(F32)
    feat_ref[FEATS:CHIP, :] = grad_ref[...].astype(F32)
    feats = feat_ref[...].astype(BF16)
    for core in range(2):
        slot = iota((experts, HALF, count), 1).astype(F32) + float(HALF * core)
        picked = code[:, None, :] == slot
        select = jnp.where(picked, 1.0, 0.0).reshape(half, count).astype(BF16)
        slot_weight = jnp.sum(
            jnp.where(picked, weight[:, None, :], 0.0).reshape(half, count), axis=1, keepdims=True
        )
        rows = lax.dot_general(select, feats, NT, preferred_element_type=F32)
        rows = jnp.where(iota(rows.shape, 1) == CHIP, slot_weight, rows)
        sel_ref[core * half : (core + 1) * half, :] = select
        rows_ref[core * half : (core + 1) * half, :] = rows.astype(BF16)


def join_kernel(parts_ref, rows_ref):
    first, second = parts_ref[0].astype(F32), parts_ref[1].astype(F32)
    rest = first[:, CHIP:WIDE]
    tok = jnp.concatenate([first[:, :FEATS], second[:, :FEATS], rest], axis=1)
    grad = jnp.concatenate([first[:, FEATS:CHIP], second[:, FEATS:CHIP], rest], axis=1)
    rows_ref[:, :WIDE] = tok.astype(BF16)
    rows_ref[:, WIDE:] = grad.astype(BF16)


def pack_kernel(gate_ref, up_ref, down_ref, out_ref, source, packed, sems_in, sems_out):
    chips = packed.shape[0]
    loads = [
        pltpu.make_async_copy(ref, source.at[part], sems_in.at[part])
        for part, ref in enumerate((gate_ref, up_ref, down_ref))
    ]
    for load in loads:
        load.start()
    spare = HID - HIDDEN
    spot = iota((spare, WIDE), 1) == iota((spare, WIDE), 0) + CHIP
    mark = jnp.where(jnp.logical_and(spot, iota((spare, WIDE), 0) < 2), 1.0, 0.0)
    stores = []
    for part in range(3):
        loads[part].wait()
        for chip in range(chips):
            start = chip * CHIP
            low = start // 128 * 128
            high = min(low + 512, source.shape[2])
            w = source[part, :, low:high].astype(F32)
            w = w[:, start - low : start - low + CHIP]
            w = jnp.concatenate([w, jnp.zeros((HIDDEN, WIDE - CHIP), F32)], axis=1)
            tail = mark if part == 0 else jnp.zeros_like(mark)
            w = jnp.concatenate([w, tail], axis=0)
            packed[chip, part * HID : (part + 1) * HID, :] = w.astype(BF16)
        rows = pl.ds(part * HID, HID)
        stores.append(
            pltpu.make_async_copy(
                packed.at[:, rows, :], out_ref.at[:, rows, :], sems_out.at[part]
            )
        )
        stores[part].start()
    for store in stores:
        store.wait()


def project(w, rows, total):
    fresh = (
        lax.dot_general(w[: 2 * HID, :], rows[:, :WIDE], NT, preferred_element_type=F32),
        lax.dot_general(w[2 * HID :, :], rows[:, WIDE:], NT, preferred_element_type=F32),
    )
    return fresh if total is None else (total[0] + fresh[0], total[1] + fresh[1])


def chip_of(me_ref, distance, chips):
    me = me_ref[0]
    return lax.rem(me // 2 + distance * (1 - 2 * lax.rem(me, 2)) + chips, chips)


def forward_kernel(places, me_ref, *refs):
    count = len(places)
    blocks, weights, sources, sums = refs[:count], refs[count : count + 2], refs[count + 2 : -2], refs[-2:]
    chips = weights[0].shape[0]
    totals = [(ref[: 2 * HID, :], ref[2 * HID :, :]) for ref in sources] or [None, None]
    for ref, place in zip(blocks, places):
        chip = chip_of(me_ref, place, chips)
        for i in range(2):
            totals[i] = project(weights[i][chip], ref[...], totals[i])
    for i in range(2):
        sums[i][: 2 * HID, :] = totals[i][0]
        sums[i][2 * HID :, :] = totals[i][1]


def backward_kernel(
    places, me_ref, first_ref, second_ref, own_w, peer_w, own_sum, peer_sum, out_ref, terms
):
    weights = own_w, peer_w
    chips = own_w.shape[0]
    totals = [(ref[: 2 * HID, :], ref[2 * HID :, :]) for ref in (own_sum, peer_sum)]
    for ref, place in zip((first_ref, second_ref), places):
        chip = chip_of(me_ref, place, chips)
        for i in range(2):
            totals[i] = project(weights[i][chip], ref[...], totals[i])
    grads, probs = [], []
    for pre, back in totals:
        pre_gate, pre_up = pre[:HID], pre[HID:]
        weight = pre_gate[HIDDEN : HIDDEN + 1] * (1.0 / chips)
        sig = jax.nn.sigmoid(pre_gate)
        act = pre_gate * sig
        live = iota(act.shape, 0) < HIDDEN
        probs.append(jnp.sum(jnp.where(live, back * (act * pre_up), 0.0), axis=0, keepdims=True))
        hid_grad = weight * back
        d_gate = hid_grad * pre_up * sig * (1.0 + pre_gate * (1.0 - sig))
        d_up = hid_grad * act
        grads.append([jnp.where(live, d_gate, 0.0), jnp.where(live, d_up, 0.0)])
    prob = probs[0] + probs[1]
    high = prob.astype(BF16).astype(F32)
    row = iota(grads[0][0].shape, 0)
    d_gate = jnp.where(row == HIDDEN, high, grads[0][0])
    grads[0][0] = jnp.where(row == HIDDEN + 1, prob - high, d_gate)
    grads = [jnp.concatenate(g, axis=0).astype(BF16) for g in grads]
    for k in range(chips):
        value = None
        for i in range(2):
            term = lax.dot_general(
                weights[i][k, : 2 * HID, :], grads[i], TN, preferred_element_type=F32
            )
            value = term if value is None else value + term
        for part in range(2):
            start = (2 * k + part) * BACK
            terms[start : start + FEATS, :] = value[part * FEATS : (part + 1) * FEATS, :]
            terms[start + FEATS : start + BACK, :] = value[CHIP : CHIP + 2, :]
    out_ref[...] = terms[...].astype(BF16)


def combine_kernel(ret_ref, sel_ref, ids_ref, tok_ref, gate_ref):
    slots, count = sel_ref.shape
    experts = slots // CAP
    ret = ret_ref[...]
    select = sel_ref[...]
    total = lax.dot_general(ret, select, TN, preferred_element_type=F32)
    tok_ref[...] = total[:FEATS, :].astype(BF16)
    prob = ret[:, FEATS : FEATS + 1].astype(F32) + ret[:, FEATS + 1 : FEATS + 2].astype(F32)
    spread = (select.astype(F32) * prob).reshape(2, experts, HALF, count)
    per_expert = jnp.sum(spread[0] + spread[1], axis=1)
    expert = iota((experts, count), 0)
    for k in range(TOP):
        named = ids_ref[k : k + 1, :] == expert
        gate_ref[k : k + 1, :] = jnp.sum(
            jnp.where(named, per_expert, 0.0), axis=0, keepdims=True
        )


VMEM = pl.BlockSpec(memory_space=pltpu.VMEM)
SMEM = pl.BlockSpec(memory_space=pltpu.SMEM)
HBM = pl.BlockSpec(memory_space=pltpu.HBM)
DMA = pltpu.SemaphoreType.DMA
SMALL = pltpu.CompilerParams(vmem_limit_bytes=16 * 1024 * 1024)
LARGE = pltpu.CompilerParams(vmem_limit_bytes=32 * 1024 * 1024)


def after(*values):
    return lax.optimization_barrier(values)


def per_device(tokens, out_grad, expert_ids, gate_values, w_gate, w_up, w_down):
    experts = lax.axis_size("ex")
    groups = lax.axis_size("grp")
    chips = groups // 2
    slots = experts * HALF
    count = tokens.shape[0]
    me_arg = lax.axis_index("grp").astype(jnp.int32).reshape(1)
    swap = [(i, i ^ 1) for i in range(groups)]
    up = [(i, (i + 2 - 4 * (i % 2)) % groups) for i in range(groups)]
    cross = [(s ^ 1, t) for s, t in up]
    leave = [(s, t ^ 1) for s, t in up]
    both_cores = [list(range(2 * z * experts, 2 * (z + 1) * experts)) for z in range(chips)]
    ids, me_arg = after(expert_ids.T, me_arg)

    def exchange(rows):
        return lax.all_to_all(
            rows.reshape(2 * experts, HALF, rows.shape[-1]),
            ("grp", "ex"),
            split_axis=0,
            concat_axis=0,
            axis_index_groups=both_cores,
            tiled=True,
        )

    rows, select = pl.pallas_call(
        dispatch_kernel,
        in_specs=[VMEM] * 4,
        out_shape=(
            jax.ShapeDtypeStruct((2 * slots, WIDE), BF16),
            jax.ShapeDtypeStruct((2 * slots, count), BF16),
        ),
        scratch_shapes=[pltpu.VMEM((WIDE, count), F32)],
        compiler_params=SMALL,
        name="dispatch",
    )(ids, gate_values.T, tokens.T, out_grad.T)
    own_w = pl.pallas_call(
        pack_kernel,
        in_specs=[HBM] * 3,
        out_specs=HBM,
        out_shape=jax.ShapeDtypeStruct((chips, 3 * HID, WIDE), BF16),
        scratch_shapes=[
            pltpu.VMEM((3,) + w_gate.shape[1:], BF16),
            pltpu.VMEM((chips, 3 * HID, WIDE), BF16),
            DMA((3,)),
            DMA((3,)),
        ],
        compiler_params=pltpu.CompilerParams(vmem_limit_bytes=60 * 1024 * 1024),
        name="pack",
    )(w_gate[0], w_up[0], w_down[0])
    rows, own_w = after(rows, own_w)
    rows = pl.pallas_call(
        join_kernel,
        in_specs=[VMEM],
        out_specs=VMEM,
        out_shape=jax.ShapeDtypeStruct((slots, 2 * WIDE), BF16),
        compiler_params=SMALL,
        name="join",
    )(exchange(rows).reshape(2, slots, WIDE))

    rows, own_w = after(rows, own_w)
    peer_w = lax.ppermute(own_w, "grp", swap)
    def forward(blocks, places, sums):
        n = len(blocks)
        return pl.pallas_call(
            functools.partial(forward_kernel, places),
            in_specs=[SMEM] + [VMEM] * (n + 2 + len(sums)),
            out_specs=[VMEM] * 2,
            out_shape=[jax.ShapeDtypeStruct((3 * HID, slots), F32)] * 2,
            compiler_params=LARGE,
            cost_estimate=pl.CostEstimate(
                flops=n * 4 * slots * 3 * HID * WIDE,
                bytes_accessed=n * (slots + 3 * HID) * 4 * WIDE + 8 * 3 * HID * slots,
                transcendentals=0,
            ),
            name="forward",
        )(me_arg, *blocks, own_w, peer_w, *sums)

    mine1 = lax.ppermute(rows, "grp", up)
    other1 = lax.ppermute(rows, "grp", cross)
    mine2 = lax.ppermute(mine1, "grp", up)
    other2 = lax.ppermute(other1, "grp", up)
    other1, mine2 = after(other1, mine2)
    came1 = lax.ppermute(other1, "grp", swap)
    mine3 = lax.ppermute(mine2, "grp", up)
    sums = forward([rows, mine1], (0, -1), ())
    other2, sums = after(other2, sums)
    other3 = lax.ppermute(other2, "grp", up)
    came4 = lax.ppermute(other3, "grp", leave)
    other2, other3 = after(other2, other3)
    came2 = lax.ppermute(other2, "grp", swap)
    came3 = lax.ppermute(other3, "grp", swap)

    sums = forward([mine2, came1], (-2, 1), sums)
    sums = forward([mine3, came4], (-3, 4), sums)
    terms = pl.pallas_call(
        functools.partial(backward_kernel, (2, 3)),
        in_specs=[SMEM] + [VMEM] * 6,
        out_specs=VMEM,
        out_shape=jax.ShapeDtypeStruct((groups * BACK, slots), BF16),
        scratch_shapes=[pltpu.VMEM((groups * BACK, slots), F32)],
        compiler_params=LARGE,
        name="backward",
    )(me_arg, came2, came3, own_w, peer_w, *sums)

    same_core = [list(range(c, groups, 2)) for c in range(2)]
    part = lax.psum_scatter(
        terms, "grp", scatter_dimension=0, axis_index_groups=same_core, tiled=True
    )
    ret = exchange(part.reshape(2, BACK, slots).transpose(0, 2, 1)).reshape(2 * slots, BACK)
    tok, gate = pl.pallas_call(
        combine_kernel,
        in_specs=[VMEM] * 3,
        out_shape=(
            jax.ShapeDtypeStruct((FEATS, count), BF16),
            jax.ShapeDtypeStruct((TOP, count), F32),
        ),
        compiler_params=SMALL,
        name="combine",
    )(ret, select, ids)
    return tok.T, gate.T


def solution(mesh):
    return jax.shard_map(
        per_device,
        mesh=mesh,
        in_specs=(
            P("ex", "grp"),
            P("ex", "grp"),
            P("ex", None),
            P("ex", None),
            P("ex", "grp", None),
            P("ex", "grp", None),
            P("ex", "grp", None),
        ),
        out_specs=(P("ex", "grp"), P("ex", None)),
        check_vma=False,
    )
```

```python
import functools

import jax
import jax.numpy as jnp
from jax import lax
from jax.experimental import pallas as pl
from jax.experimental.pallas import tpu as pltpu
from jax.sharding import PartitionSpec as P

TOP = 4
CAP = 16
HALF = CAP // 2
FEATS = 180
HIDDEN = 180
HID = 192
WIDE = 384
CHIP = 2 * FEATS
BACK = FEATS + 2
NT = (((1,), (1,)), ((), ()))
TN = (((0,), (0,)), ((), ()))
F32 = jnp.float32
BF16 = jnp.bfloat16


def iota(shape, dim):
    return lax.broadcasted_iota(jnp.int32, shape, dim)


def dispatch_kernel(ids_ref, gate_ref, tok_ref, grad_ref, rows_ref, sel_ref, feat_ref):
    slots, count = sel_ref.shape
    half = slots // 2
    experts = half // HALF
    gates = gate_ref[...].astype(F32)
    expert = iota((experts, count), 0)
    member = jnp.zeros((experts, count), F32)
    weight = jnp.zeros((experts, count), F32)
    for k in range(TOP):
        named = ids_ref[k : k + 1, :] == expert
        member = jnp.where(named, 1.0, member)
        weight = jnp.where(named, gates[k : k + 1, :], weight)
    earlier = jnp.where(iota((count, count), 0) < iota((count, count), 1), 1.0, 0.0)
    place = jnp.dot(member.astype(BF16), earlier.astype(BF16), preferred_element_type=F32)
    code = jnp.where(member > 0.0, place, -1.0)
    feat_ref[...] = jnp.zeros_like(feat_ref)
    feat_ref[:FEATS, :] = tok_ref[...].astype(F32)
    feat_ref[FEATS:CHIP, :] = grad_ref[...].astype(F32)
    feats = feat_ref[...].astype(BF16)
    for core in range(2):
        slot = iota((experts, HALF, count), 1).astype(F32) + float(HALF * core)
        picked = code[:, None, :] == slot
        select = jnp.where(picked, 1.0, 0.0).reshape(half, count).astype(BF16)
        slot_weight = jnp.sum(
            jnp.where(picked, weight[:, None, :], 0.0).reshape(half, count), axis=1, keepdims=True
        )
        rows = lax.dot_general(select, feats, NT, preferred_element_type=F32)
        rows = jnp.where(iota(rows.shape, 1) == CHIP, slot_weight, rows)
        sel_ref[core * half : (core + 1) * half, :] = select
        rows_ref[core * half : (core + 1) * half, :] = rows.astype(BF16)


def join_kernel(parts_ref, rows_ref):
    first, second = parts_ref[0].astype(F32), parts_ref[1].astype(F32)
    rest = first[:, CHIP:WIDE]
    tok = jnp.concatenate([first[:, :FEATS], second[:, :FEATS], rest], axis=1)
    grad = jnp.concatenate([first[:, FEATS:CHIP], second[:, FEATS:CHIP], rest], axis=1)
    rows_ref[:, :WIDE] = tok.astype(BF16)
    rows_ref[:, WIDE:] = grad.astype(BF16)


def pack_kernel(gate_ref, up_ref, down_ref, out_ref, source, packed, sems_in, sems_out):
    chips = packed.shape[0]
    loads = [
        pltpu.make_async_copy(ref, source.at[part], sems_in.at[part])
        for part, ref in enumerate((gate_ref, up_ref, down_ref))
    ]
    for load in loads:
        load.start()
    spare = HID - HIDDEN
    spot = iota((spare, WIDE), 1) == iota((spare, WIDE), 0) + CHIP
    mark = jnp.where(jnp.logical_and(spot, iota((spare, WIDE), 0) < 2), 1.0, 0.0)
    stores = []
    for part in range(3):
        loads[part].wait()
        for chip in range(chips):
            start = chip * CHIP
            low = start // 128 * 128
            high = min(low + 512, source.shape[2])
            w = source[part, :, low:high].astype(F32)
            w = w[:, start - low : start - low + CHIP]
            w = jnp.concatenate([w, jnp.zeros((HIDDEN, WIDE - CHIP), F32)], axis=1)
            tail = mark if part == 0 else jnp.zeros_like(mark)
            w = jnp.concatenate([w, tail], axis=0)
            packed[chip, part * HID : (part + 1) * HID, :] = w.astype(BF16)
        rows = pl.ds(part * HID, HID)
        stores.append(
            pltpu.make_async_copy(
                packed.at[:, rows, :], out_ref.at[:, rows, :], sems_out.at[part]
            )
        )
        stores[part].start()
    for store in stores:
        store.wait()


def project(w, rows, total):
    fresh = (
        lax.dot_general(w[: 2 * HID, :], rows[:, :WIDE], NT, preferred_element_type=F32),
        lax.dot_general(w[2 * HID :, :], rows[:, WIDE:], NT, preferred_element_type=F32),
    )
    return fresh if total is None else (total[0] + fresh[0], total[1] + fresh[1])


def chip_of(me_ref, distance, chips):
    me = me_ref[0]
    return lax.rem(me // 2 + distance * (1 - 2 * lax.rem(me, 2)) + chips, chips)


def forward_kernel(places, me_ref, *refs):
    count = len(places)
    blocks, weights, sources, sums = refs[:count], refs[count : count + 2], refs[count + 2 : -2], refs[-2:]
    chips = weights[0].shape[0]
    totals = [(ref[: 2 * HID, :], ref[2 * HID :, :]) for ref in sources] or [None, None]
    for ref, place in zip(blocks, places):
        chip = chip_of(me_ref, place, chips)
        for i in range(2):
            totals[i] = project(weights[i][chip], ref[...], totals[i])
    for i in range(2):
        sums[i][: 2 * HID, :] = totals[i][0]
        sums[i][2 * HID :, :] = totals[i][1]


def backward_kernel(
    places, me_ref, first_ref, second_ref, own_w, peer_w, own_sum, peer_sum, out_ref
):
    weights = own_w, peer_w
    chips = own_w.shape[0]
    totals = [(ref[: 2 * HID, :], ref[2 * HID :, :]) for ref in (own_sum, peer_sum)]
    for ref, place in zip((first_ref, second_ref), places):
        chip = chip_of(me_ref, place, chips)
        for i in range(2):
            totals[i] = project(weights[i][chip], ref[...], totals[i])
    grads, probs = [], []
    for pre, back in totals:
        pre_gate, pre_up = pre[:HID], pre[HID:]
        weight = pre_gate[HIDDEN : HIDDEN + 1] * (1.0 / chips)
        sig = jax.nn.sigmoid(pre_gate)
        act = pre_gate * sig
        live = iota(act.shape, 0) < HIDDEN
        probs.append(jnp.sum(jnp.where(live, back * (act * pre_up), 0.0), axis=0, keepdims=True))
        hid_grad = weight * back
        d_gate = hid_grad * pre_up * sig * (1.0 + pre_gate * (1.0 - sig))
        d_up = hid_grad * act
        grads.append([jnp.where(live, d_gate, 0.0), jnp.where(live, d_up, 0.0)])
    prob = probs[0] + probs[1]
    high = prob.astype(BF16).astype(F32)
    row = iota(grads[0][0].shape, 0)
    d_gate = jnp.where(row == HIDDEN, high, grads[0][0])
    grads[0][0] = jnp.where(row == HIDDEN + 1, prob - high, d_gate)
    grads = [jnp.concatenate(g, axis=0).astype(BF16) for g in grads]
    grad = jnp.concatenate(grads, axis=0)
    for k in range(chips):
        w = jnp.concatenate([ref[k, : 2 * HID, :] for ref in weights], axis=0)
        value = lax.dot_general(w, grad, TN, preferred_element_type=F32).astype(BF16)
        for part in range(2):
            start = (2 * k + part) * BACK
            out_ref[start : start + FEATS, :] = value[part * FEATS : (part + 1) * FEATS, :]
            out_ref[start + FEATS : start + BACK, :] = value[CHIP : CHIP + 2, :]


def combine_kernel(ret_ref, sel_ref, ids_ref, tok_ref, gate_ref):
    slots, count = sel_ref.shape
    experts = slots // CAP
    ret = ret_ref[...]
    select = sel_ref[...]
    total = lax.dot_general(ret, select, TN, preferred_element_type=F32)
    tok_ref[...] = total[:FEATS, :].astype(BF16)
    prob = ret[:, FEATS : FEATS + 1].astype(F32) + ret[:, FEATS + 1 : FEATS + 2].astype(F32)
    spread = (select.astype(F32) * prob).reshape(2, experts, HALF, count)
    per_expert = jnp.sum(spread[0] + spread[1], axis=1)
    expert = iota((experts, count), 0)
    for k in range(TOP):
        named = ids_ref[k : k + 1, :] == expert
        gate_ref[k : k + 1, :] = jnp.sum(
            jnp.where(named, per_expert, 0.0), axis=0, keepdims=True
        )


VMEM = pl.BlockSpec(memory_space=pltpu.VMEM)
SMEM = pl.BlockSpec(memory_space=pltpu.SMEM)
HBM = pl.BlockSpec(memory_space=pltpu.HBM)
DMA = pltpu.SemaphoreType.DMA
SMALL = pltpu.CompilerParams(vmem_limit_bytes=16 * 1024 * 1024)
LARGE = pltpu.CompilerParams(vmem_limit_bytes=32 * 1024 * 1024)


def after(*values):
    return lax.optimization_barrier(values)


def per_device(tokens, out_grad, expert_ids, gate_values, w_gate, w_up, w_down):
    experts = lax.axis_size("ex")
    groups = lax.axis_size("grp")
    chips = groups // 2
    slots = experts * HALF
    count = tokens.shape[0]
    me_arg = lax.axis_index("grp").astype(jnp.int32).reshape(1)
    swap = [(i, i ^ 1) for i in range(groups)]
    up = [(i, (i + 2 - 4 * (i % 2)) % groups) for i in range(groups)]
    cross = [(s ^ 1, t) for s, t in up]
    leave = [(s, t ^ 1) for s, t in up]
    both_cores = [list(range(2 * z * experts, 2 * (z + 1) * experts)) for z in range(chips)]
    ids, me_arg = after(expert_ids.T, me_arg)

    def exchange(rows):
        return lax.all_to_all(
            rows.reshape(2 * experts, HALF, rows.shape[-1]),
            ("grp", "ex"),
            split_axis=0,
            concat_axis=0,
            axis_index_groups=both_cores,
            tiled=True,
        )

    rows, select = pl.pallas_call(
        dispatch_kernel,
        in_specs=[VMEM] * 4,
        out_shape=(
            jax.ShapeDtypeStruct((2 * slots, WIDE), BF16),
            jax.ShapeDtypeStruct((2 * slots, count), BF16),
        ),
        scratch_shapes=[pltpu.VMEM((WIDE, count), F32)],
        compiler_params=SMALL,
        name="dispatch",
    )(ids, gate_values.T, tokens.T, out_grad.T)
    own_w = pl.pallas_call(
        pack_kernel,
        in_specs=[HBM] * 3,
        out_specs=HBM,
        out_shape=jax.ShapeDtypeStruct((chips, 3 * HID, WIDE), BF16),
        scratch_shapes=[
            pltpu.VMEM((3,) + w_gate.shape[1:], BF16),
            pltpu.VMEM((chips, 3 * HID, WIDE), BF16),
            DMA((3,)),
            DMA((3,)),
        ],
        compiler_params=pltpu.CompilerParams(vmem_limit_bytes=60 * 1024 * 1024),
        name="pack",
    )(w_gate[0], w_up[0], w_down[0])
    rows, own_w = after(rows, own_w)
    rows = pl.pallas_call(
        join_kernel,
        in_specs=[VMEM],
        out_specs=VMEM,
        out_shape=jax.ShapeDtypeStruct((slots, 2 * WIDE), BF16),
        compiler_params=SMALL,
        name="join",
    )(exchange(rows).reshape(2, slots, WIDE))

    rows, own_w = after(rows, own_w)
    peer_w = lax.ppermute(own_w, "grp", swap)
    def forward(blocks, places, sums):
        n = len(blocks)
        return pl.pallas_call(
            functools.partial(forward_kernel, places),
            in_specs=[SMEM] + [VMEM] * (n + 2 + len(sums)),
            out_specs=[VMEM] * 2,
            out_shape=[jax.ShapeDtypeStruct((3 * HID, slots), F32)] * 2,
            compiler_params=LARGE,
            cost_estimate=pl.CostEstimate(
                flops=n * 4 * slots * 3 * HID * WIDE,
                bytes_accessed=n * (slots + 3 * HID) * 4 * WIDE + 8 * 3 * HID * slots,
                transcendentals=0,
            ),
            name="forward",
        )(me_arg, *blocks, own_w, peer_w, *sums)

    mine1 = lax.ppermute(rows, "grp", up)
    other1 = lax.ppermute(rows, "grp", cross)
    mine2 = lax.ppermute(mine1, "grp", up)
    other2 = lax.ppermute(other1, "grp", up)
    other1, mine2 = after(other1, mine2)
    came1 = lax.ppermute(other1, "grp", swap)
    mine3 = lax.ppermute(mine2, "grp", up)
    sums = forward([rows, mine1], (0, -1), ())
    other2, sums = after(other2, sums)
    other3 = lax.ppermute(other2, "grp", up)
    came4 = lax.ppermute(other3, "grp", leave)
    other2, other3 = after(other2, other3)
    came2 = lax.ppermute(other2, "grp", swap)
    came3 = lax.ppermute(other3, "grp", swap)

    sums = forward([mine2, came1, mine3], (-2, 1, -3), sums)
    sums = forward([came4], (4,), sums)
    terms = pl.pallas_call(
        functools.partial(backward_kernel, (2, 3)),
        in_specs=[SMEM] + [VMEM] * 6,
        out_specs=VMEM,
        out_shape=jax.ShapeDtypeStruct((groups * BACK, slots), BF16),
        compiler_params=LARGE,
        name="backward",
    )(me_arg, came2, came3, own_w, peer_w, *sums)

    same_core = [list(range(c, groups, 2)) for c in range(2)]
    part = lax.psum_scatter(
        terms, "grp", scatter_dimension=0, axis_index_groups=same_core, tiled=True
    )
    ret = exchange(part.reshape(2, BACK, slots).transpose(0, 2, 1)).reshape(2 * slots, BACK)
    tok, gate = pl.pallas_call(
        combine_kernel,
        in_specs=[VMEM] * 3,
        out_shape=(
            jax.ShapeDtypeStruct((FEATS, count), BF16),
            jax.ShapeDtypeStruct((TOP, count), F32),
        ),
        compiler_params=SMALL,
        name="combine",
    )(ret, select, ids)
    return tok.T, gate.T


def solution(mesh):
    return jax.shard_map(
        per_device,
        mesh=mesh,
        in_specs=(
            P("ex", "grp"),
            P("ex", "grp"),
            P("ex", None),
            P("ex", None),
            P("ex", "grp", None),
            P("ex", "grp", None),
            P("ex", "grp", None),
        ),
        out_specs=(P("ex", "grp"), P("ex", None)),
        check_vma=False,
    )
```

```python
import functools

import jax
import jax.numpy as jnp
from jax import lax
from jax.experimental import pallas as pl
from jax.experimental.pallas import tpu as pltpu
from jax.sharding import PartitionSpec as P

TOP = 4
CAP = 16
HALF = CAP // 2
FEATS = 180
HIDDEN = 180
HID = 192
WIDE = 384
CHIP = 2 * FEATS
BACK = FEATS + 2
NT = (((1,), (1,)), ((), ()))
TN = (((0,), (0,)), ((), ()))
F32 = jnp.float32
BF16 = jnp.bfloat16


def iota(shape, dim):
    return lax.broadcasted_iota(jnp.int32, shape, dim)


def dispatch_kernel(ids_ref, gate_ref, tok_ref, grad_ref, rows_ref, sel_ref, feat_ref):
    slots, count = sel_ref.shape
    half = slots // 2
    experts = half // HALF
    gates = gate_ref[...].astype(F32)
    expert = iota((experts, count), 0)
    member = jnp.zeros((experts, count), F32)
    weight = jnp.zeros((experts, count), F32)
    for k in range(TOP):
        named = ids_ref[k : k + 1, :] == expert
        member = jnp.where(named, 1.0, member)
        weight = jnp.where(named, gates[k : k + 1, :], weight)
    earlier = jnp.where(iota((count, count), 0) < iota((count, count), 1), 1.0, 0.0)
    place = jnp.dot(member.astype(BF16), earlier.astype(BF16), preferred_element_type=F32)
    code = jnp.where(member > 0.0, place, -1.0)
    feat_ref[...] = jnp.zeros_like(feat_ref)
    feat_ref[:FEATS, :] = tok_ref[...].astype(F32)
    feat_ref[FEATS:CHIP, :] = grad_ref[...].astype(F32)
    feats = feat_ref[...].astype(BF16)
    for core in range(2):
        slot = iota((experts, HALF, count), 1).astype(F32) + float(HALF * core)
        picked = code[:, None, :] == slot
        select = jnp.where(picked, 1.0, 0.0).reshape(half, count).astype(BF16)
        slot_weight = jnp.sum(
            jnp.where(picked, weight[:, None, :], 0.0).reshape(half, count), axis=1, keepdims=True
        )
        rows = lax.dot_general(select, feats, NT, preferred_element_type=F32)
        rows = jnp.where(iota(rows.shape, 1) == CHIP, slot_weight, rows)
        sel_ref[core * half : (core + 1) * half, :] = select
        rows_ref[core * half : (core + 1) * half, :] = rows.astype(BF16)


def join_kernel(parts_ref, rows_ref):
    first, second = parts_ref[0].astype(F32), parts_ref[1].astype(F32)
    rest = first[:, CHIP:WIDE]
    tok = jnp.concatenate([first[:, :FEATS], second[:, :FEATS], rest], axis=1)
    grad = jnp.concatenate([first[:, FEATS:CHIP], second[:, FEATS:CHIP], rest], axis=1)
    rows_ref[:, :WIDE] = tok.astype(BF16)
    rows_ref[:, WIDE:] = grad.astype(BF16)


def pack_kernel(gate_ref, up_ref, down_ref, out_ref, source, packed, sems_in, sems_out):
    chips = packed.shape[0]
    loads = [
        pltpu.make_async_copy(ref, source.at[part], sems_in.at[part])
        for part, ref in enumerate((gate_ref, up_ref, down_ref))
    ]
    for load in loads:
        load.start()
    spare = HID - HIDDEN
    spot = iota((spare, WIDE), 1) == iota((spare, WIDE), 0) + CHIP
    mark = jnp.where(jnp.logical_and(spot, iota((spare, WIDE), 0) < 2), 1.0, 0.0)
    stores = []
    for part in range(3):
        loads[part].wait()
        for chip in range(chips):
            start = chip * CHIP
            low = start // 128 * 128
            high = min(low + 512, source.shape[2])
            w = source[part, :, low:high].astype(F32)
            w = w[:, start - low : start - low + CHIP]
            w = jnp.concatenate([w, jnp.zeros((HIDDEN, WIDE - CHIP), F32)], axis=1)
            tail = mark if part == 0 else jnp.zeros_like(mark)
            w = jnp.concatenate([w, tail], axis=0)
            packed[chip, part * HID : (part + 1) * HID, :] = w.astype(BF16)
        rows = pl.ds(part * HID, HID)
        stores.append(
            pltpu.make_async_copy(
                packed.at[:, rows, :], out_ref.at[:, rows, :], sems_out.at[part]
            )
        )
        stores[part].start()
    for store in stores:
        store.wait()


def project(w, rows, total):
    fresh = (
        lax.dot_general(w[: 2 * HID, :], rows[:, :WIDE], NT, preferred_element_type=F32),
        lax.dot_general(w[2 * HID :, :], rows[:, WIDE:], NT, preferred_element_type=F32),
    )
    return fresh if total is None else (total[0] + fresh[0], total[1] + fresh[1])


def chip_of(me_ref, distance, chips):
    me = me_ref[0]
    return lax.rem(me // 2 + distance * (1 - 2 * lax.rem(me, 2)) + chips, chips)


def forward_kernel(places, me_ref, *refs):
    count = len(places)
    blocks, weights, sources, sums = refs[:count], refs[count : count + 2], refs[count + 2 : -2], refs[-2:]
    chips = weights[0].shape[0]
    totals = [(ref[: 2 * HID, :], ref[2 * HID :, :]) for ref in sources] or [None, None]
    for ref, place in zip(blocks, places):
        chip = chip_of(me_ref, place, chips)
        for i in range(2):
            totals[i] = project(weights[i][chip], ref[...], totals[i])
    for i in range(2):
        sums[i][: 2 * HID, :] = totals[i][0]
        sums[i][2 * HID :, :] = totals[i][1]


def backward_kernel(
    places, me_ref, first_ref, second_ref, own_w, peer_w, own_sum, peer_sum, out_ref, terms
):
    weights = own_w, peer_w
    chips = own_w.shape[0]
    totals = [(ref[: 2 * HID, :], ref[2 * HID :, :]) for ref in (own_sum, peer_sum)]
    for ref, place in zip((first_ref, second_ref), places):
        chip = chip_of(me_ref, place, chips)
        for i in range(2):
            totals[i] = project(weights[i][chip], ref[...], totals[i])
    grads, probs = [], []
    for pre, back in totals:
        pre_gate, pre_up = pre[:HID], pre[HID:]
        weight = pre_gate[HIDDEN : HIDDEN + 1] * (1.0 / chips)
        sig = jax.nn.sigmoid(pre_gate)
        act = pre_gate * sig
        live = iota(act.shape, 0) < HIDDEN
        probs.append(jnp.sum(jnp.where(live, back * (act * pre_up), 0.0), axis=0, keepdims=True))
        hid_grad = weight * back
        d_gate = hid_grad * pre_up * sig * (1.0 + pre_gate * (1.0 - sig))
        d_up = hid_grad * act
        grads.append([jnp.where(live, d_gate, 0.0), jnp.where(live, d_up, 0.0)])
    prob = probs[0] + probs[1]
    high = prob.astype(BF16).astype(F32)
    row = iota(grads[0][0].shape, 0)
    d_gate = jnp.where(row == HIDDEN, high, grads[0][0])
    grads[0][0] = jnp.where(row == HIDDEN + 1, prob - high, d_gate)
    grads = [jnp.concatenate(g, axis=0).astype(BF16) for g in grads]
    grad = jnp.concatenate(grads, axis=0)
    for k in range(chips):
        w = jnp.concatenate([ref[k, : 2 * HID, :] for ref in weights], axis=0)
        value = lax.dot_general(w, grad, TN, preferred_element_type=F32)
        for part in range(2):
            start = (2 * k + part) * BACK
            terms[start : start + FEATS, :] = value[part * FEATS : (part + 1) * FEATS, :]
            terms[start + FEATS : start + BACK, :] = value[CHIP : CHIP + 2, :]
    out_ref[...] = terms[...].astype(BF16)


def combine_kernel(ret_ref, sel_ref, ids_ref, tok_ref, gate_ref):
    slots, count = sel_ref.shape
    experts = slots // CAP
    ret = ret_ref[...]
    select = sel_ref[...]
    total = lax.dot_general(ret, select, TN, preferred_element_type=F32)
    tok_ref[...] = total[:FEATS, :].astype(BF16)
    prob = ret[:, FEATS : FEATS + 1].astype(F32) + ret[:, FEATS + 1 : FEATS + 2].astype(F32)
    spread = (select.astype(F32) * prob).reshape(2, experts, HALF, count)
    per_expert = jnp.sum(spread[0] + spread[1], axis=1)
    expert = iota((experts, count), 0)
    for k in range(TOP):
        named = ids_ref[k : k + 1, :] == expert
        gate_ref[k : k + 1, :] = jnp.sum(
            jnp.where(named, per_expert, 0.0), axis=0, keepdims=True
        )


VMEM = pl.BlockSpec(memory_space=pltpu.VMEM)
SMEM = pl.BlockSpec(memory_space=pltpu.SMEM)
HBM = pl.BlockSpec(memory_space=pltpu.HBM)
DMA = pltpu.SemaphoreType.DMA
SMALL = pltpu.CompilerParams(vmem_limit_bytes=16 * 1024 * 1024)
LARGE = pltpu.CompilerParams(vmem_limit_bytes=32 * 1024 * 1024)


def after(*values):
    return lax.optimization_barrier(values)


def per_device(tokens, out_grad, expert_ids, gate_values, w_gate, w_up, w_down):
    experts = lax.axis_size("ex")
    groups = lax.axis_size("grp")
    chips = groups // 2
    slots = experts * HALF
    count = tokens.shape[0]
    me_arg = lax.axis_index("grp").astype(jnp.int32).reshape(1)
    swap = [(i, i ^ 1) for i in range(groups)]
    up = [(i, (i + 2 - 4 * (i % 2)) % groups) for i in range(groups)]
    cross = [(s ^ 1, t) for s, t in up]
    leave = [(s, t ^ 1) for s, t in up]
    both_cores = [list(range(2 * z * experts, 2 * (z + 1) * experts)) for z in range(chips)]
    ids, me_arg = after(expert_ids.T, me_arg)

    def exchange(rows):
        return lax.all_to_all(
            rows.reshape(2 * experts, HALF, rows.shape[-1]),
            ("grp", "ex"),
            split_axis=0,
            concat_axis=0,
            axis_index_groups=both_cores,
            tiled=True,
        )

    rows, select = pl.pallas_call(
        dispatch_kernel,
        in_specs=[VMEM] * 4,
        out_shape=(
            jax.ShapeDtypeStruct((2 * slots, WIDE), BF16),
            jax.ShapeDtypeStruct((2 * slots, count), BF16),
        ),
        scratch_shapes=[pltpu.VMEM((WIDE, count), F32)],
        compiler_params=SMALL,
        name="dispatch",
    )(ids, gate_values.T, tokens.T, out_grad.T)
    own_w = pl.pallas_call(
        pack_kernel,
        in_specs=[HBM] * 3,
        out_specs=HBM,
        out_shape=jax.ShapeDtypeStruct((chips, 3 * HID, WIDE), BF16),
        scratch_shapes=[
            pltpu.VMEM((3,) + w_gate.shape[1:], BF16),
            pltpu.VMEM((chips, 3 * HID, WIDE), BF16),
            DMA((3,)),
            DMA((3,)),
        ],
        compiler_params=pltpu.CompilerParams(vmem_limit_bytes=60 * 1024 * 1024),
        name="pack",
    )(w_gate[0], w_up[0], w_down[0])
    rows, own_w = after(rows, own_w)
    rows = pl.pallas_call(
        join_kernel,
        in_specs=[VMEM],
        out_specs=VMEM,
        out_shape=jax.ShapeDtypeStruct((slots, 2 * WIDE), BF16),
        compiler_params=SMALL,
        name="join",
    )(exchange(rows).reshape(2, slots, WIDE))

    rows, own_w = after(rows, own_w)
    peer_w = lax.ppermute(own_w, "grp", swap)
    def forward(blocks, places, sums):
        n = len(blocks)
        return pl.pallas_call(
            functools.partial(forward_kernel, places),
            in_specs=[SMEM] + [VMEM] * (n + 2 + len(sums)),
            out_specs=[VMEM] * 2,
            out_shape=[jax.ShapeDtypeStruct((3 * HID, slots), F32)] * 2,
            compiler_params=LARGE,
            cost_estimate=pl.CostEstimate(
                flops=n * 4 * slots * 3 * HID * WIDE,
                bytes_accessed=n * (slots + 3 * HID) * 4 * WIDE + 8 * 3 * HID * slots,
                transcendentals=0,
            ),
            name="forward",
        )(me_arg, *blocks, own_w, peer_w, *sums)

    mine1 = lax.ppermute(rows, "grp", up)
    other1 = lax.ppermute(rows, "grp", cross)
    mine2 = lax.ppermute(mine1, "grp", up)
    other2 = lax.ppermute(other1, "grp", up)
    other1, mine2 = after(other1, mine2)
    came1 = lax.ppermute(other1, "grp", swap)
    mine3 = lax.ppermute(mine2, "grp", up)
    sums = forward([rows, mine1], (0, -1), ())
    other2, sums = after(other2, sums)
    other3 = lax.ppermute(other2, "grp", up)
    came4 = lax.ppermute(other3, "grp", leave)
    other2, other3 = after(other2, other3)
    came2 = lax.ppermute(other2, "grp", swap)
    came3 = lax.ppermute(other3, "grp", swap)

    sums = forward([mine2, came1, mine3], (-2, 1, -3), sums)
    sums = forward([came4], (4,), sums)
    terms = pl.pallas_call(
        functools.partial(backward_kernel, (2, 3)),
        in_specs=[SMEM] + [VMEM] * 6,
        out_specs=VMEM,
        out_shape=jax.ShapeDtypeStruct((groups * BACK, slots), BF16),
        scratch_shapes=[pltpu.VMEM((groups * BACK, slots), F32)],
        compiler_params=LARGE,
        name="backward",
    )(me_arg, came2, came3, own_w, peer_w, *sums)

    same_core = [list(range(c, groups, 2)) for c in range(2)]
    part = lax.psum_scatter(
        terms, "grp", scatter_dimension=0, axis_index_groups=same_core, tiled=True
    )
    ret = exchange(part.reshape(2, BACK, slots).transpose(0, 2, 1)).reshape(2 * slots, BACK)
    tok, gate = pl.pallas_call(
        combine_kernel,
        in_specs=[VMEM] * 3,
        out_shape=(
            jax.ShapeDtypeStruct((FEATS, count), BF16),
            jax.ShapeDtypeStruct((TOP, count), F32),
        ),
        compiler_params=SMALL,
        name="combine",
    )(ret, select, ids)
    return tok.T, gate.T


def solution(mesh):
    return jax.shard_map(
        per_device,
        mesh=mesh,
        in_specs=(
            P("ex", "grp"),
            P("ex", "grp"),
            P("ex", None),
            P("ex", None),
            P("ex", "grp", None),
            P("ex", "grp", None),
            P("ex", "grp", None),
        ),
        out_specs=(P("ex", "grp"), P("ex", None)),
        check_vma=False,
    )
```
